256 devices in a mesh: row: 16 (over y_hi, z), col: 16 (over x, y_lo, core).
Axes of the slice: x: 4, y: 4 (y_hi: 2, y_lo: 2; y = y_hi * 2 + y_lo), z: 8, core: 2. Of those that a mesh axis runs over, the one named last changes fastest.
Arguments:
- template_pair: bfloat16 [2, 64, 1280, 1280], P(None, None, ('row', 'col')), may hold values from -6 to 6
- pair_mask: int32 [1280, 1280], P(('row', 'col')), may hold values 0 or 1
- template_mask: int32 [2, 1280], replicated, may hold values 0 or 1
- in_gain: float32 [64], replicated, may hold values from 0.1 to 1.9
- proj_weight: bfloat16 [64, 256], replicated, may hold values from -0.75 to 0.75
- gate_weight: bfloat16 [64, 64], replicated, may hold values from -0.75 to 0.75
- mid_gain: float32 [64], replicated, may hold values from 0.1 to 1.9
- out_weight: bfloat16 [64, 64], replicated, may hold values from -0.75 to 0.75
- trans_gain: float32 [64], replicated, may hold values from 0.1 to 1.9
- up_weight: bfloat16 [64, 128], replicated, may hold values from -0.75 to 0.75
- down_weight: bfloat16 [128, 64], replicated, may hold values from -0.5 to 0.5
- final_gain: float32 [64], replicated, may hold values from 0.1 to 1.9
- embed_weight: bfloat16 [64, 128], replicated, may hold values from -0.75 to 0.75
Outputs:
- pair_update: bfloat16 [1280, 1280, 128], P(('row', 'col'))
The draws below stay inside these ranges and needn't reach their ends.
All inputs are finite; a program needn't handle non-finite values. No bound on the sum of `pair_mask` on one device may be relied on, other than what follows from the above.
Results may differ from the reference program's by a relative error of at most 0.0063.
Values may be sent and summed in bfloat16 or wider, within the bound.
A program may use at most 128 MiB of HBM per device.

```python
import jax
import jax.numpy as jnp
from jax import lax

C = 64
H = 128
P_SIZE = 128
TEMPLATES = 2
L = 1280


def touch_ends(entries, key, smallest, high):
    place = [jax.random.randint(jax.random.fold_in(key, axis), (), 0, length) for axis, length in enumerate(entries.shape)]
    widest = entries.shape.index(max(entries.shape))
    next_to = place[:widest] + [(place[widest] + 1) % entries.shape[widest]] + place[widest + 1:]
    return entries.at[tuple(place)].set(smallest).at[tuple(next_to)].set(high)


def steps_of(key, shape, cuts, smallest, high):
    factor_of, own = 1.0, jax.random.fold_in(key, 6)
    for position, parts in cuts:
        draws = jnp.exp(jax.random.uniform(jax.random.fold_in(own, position), (parts,), jnp.float32, smallest / len(cuts), high / len(cuts)))
        factor_of = factor_of * jnp.repeat(draws, shape[position] // parts).reshape([-1 if axis == position else 1 for axis in range(len(shape))])
    return factor_of


def bell_draw(key, dims, width, limit, cuts=(), kind=jnp.bfloat16):
    result = jax.random.normal(key, dims, jnp.float32) * width
    if len(cuts) > 0:
        result = steps_of(key, dims, cuts, -0.22, 0.18) * result
    return jnp.clip(result, min=-limit, max=limit).astype(kind)


def setup_inputs(seed: int = 0) -> dict:
    arg_keys = jax.random.split(jax.random.key(seed), 14)
    template_pair = bell_draw(arg_keys[0], (TEMPLATES, C, L, L), 1.0, 6.0, ((2, 256),))
    pair_mask = touch_ends((jax.random.randint(arg_keys[1], (L, L), 0, 10) < 9).astype(jnp.int32), jax.random.fold_in(arg_keys[1], 1), 0, 1)
    template_mask = touch_ends((jax.random.randint(arg_keys[2], (TEMPLATES, L), 0, 4) < 3).astype(jnp.int32), jax.random.fold_in(arg_keys[2], 1), 0, 1)
    in_gain = jnp.clip(1.0 + 0.18 * jax.random.normal(arg_keys[3], (C,), jnp.float32), 0.1, 1.9)
    proj_weight = bell_draw(arg_keys[4], (C, 4 * C), C ** -0.5, 0.75)
    gate_weight = bell_draw(arg_keys[5], (C, C), C ** -0.5, 0.75)
    mid_gain = jnp.clip(1.0 + 0.18 * jax.random.normal(arg_keys[6], (C,), jnp.float32), 0.1, 1.9)
    out_weight = bell_draw(arg_keys[7], (C, C), C ** -0.5, 0.75)
    trans_gain = jnp.clip(1.0 + 0.18 * jax.random.normal(arg_keys[8], (C,), jnp.float32), 0.1, 1.9)
    up_weight = bell_draw(arg_keys[9], (C, H), C ** -0.5, 0.75)
    down_weight = bell_draw(arg_keys[10], (H, C), H ** -0.5, 0.5)
    final_gain = jnp.clip(1.0 + 0.18 * jax.random.normal(arg_keys[11], (C,), jnp.float32), 0.1, 1.9)
    embed_weight = bell_draw(arg_keys[12], (C, P_SIZE), C ** -0.5, 0.75)
    return {"template_pair": template_pair, "pair_mask": pair_mask, "template_mask": template_mask, "in_gain": in_gain, "proj_weight": proj_weight, "gate_weight": gate_weight, "mid_gain": mid_gain, "out_weight": out_weight, "trans_gain": trans_gain, "up_weight": up_weight, "down_weight": down_weight, "final_gain": final_gain, "embed_weight": embed_weight}


EPSILON = 1e-05

def channel_norm(values, gain_vector):
    centre = values - lax.optimization_barrier(jnp.mean(values, axis=0, keepdims=True))
    spread = lax.optimization_barrier(jnp.mean(centre * centre, axis=0, keepdims=True))
    return centre * lax.rsqrt(spread + EPSILON) * gain_vector[:, None, None]

def project(values, weight):
    return jnp.einsum('cij,ce->eij', values.astype(jnp.float32), weight.astype(jnp.float32))

def reference(template_pair, pair_mask, template_mask, in_gain, proj_weight, gate_weight, mid_gain, out_weight, trans_gain, up_weight, down_weight, final_gain, embed_weight):
    channels = template_pair.shape[1]
    pair_weight = pair_mask.astype(jnp.float32)[None]
    mask_values = template_mask.astype(jnp.float32)
    summed = jnp.zeros(template_pair.shape[1:], jnp.float32)
    counted = jnp.zeros(template_pair.shape[2:], jnp.float32)
    for template in range(TEMPLATES):
        pair_wide = template_pair[template].astype(jnp.float32)
        normed = channel_norm(pair_wide, in_gain).astype(jnp.bfloat16)
        left_side = (jax.nn.sigmoid(project(normed, proj_weight[:, channels:2 * channels])) * project(normed, proj_weight[:, :channels]) * pair_weight).astype(jnp.bfloat16)
        right_side = (jax.nn.sigmoid(project(normed, proj_weight[:, 3 * channels:])) * project(normed, proj_weight[:, 2 * channels:3 * channels]) * pair_weight).astype(jnp.bfloat16)
        gate_value = jax.nn.sigmoid(project(normed, gate_weight))
        triangle = jnp.einsum('cik,cjk->cij', left_side.astype(jnp.float32), right_side.astype(jnp.float32)).astype(jnp.bfloat16)
        tri_normed = channel_norm(triangle.astype(jnp.float32), mid_gain).astype(jnp.bfloat16)
        updated = pair_wide + gate_value * project(tri_normed, out_weight)
        trans_in = channel_norm(updated, trans_gain).astype(jnp.bfloat16)
        hidden = jax.nn.relu(project(trans_in, up_weight)).astype(jnp.bfloat16)
        stacked = updated + project(hidden, down_weight)
        final = channel_norm(stacked, final_gain)
        coverage = mask_values[template][:, None] * mask_values[template][None, :]
        summed = summed + coverage[None] * final
        counted = counted + coverage
    averaged = summed / jnp.maximum(counted, 1.0)[None]
    activated = jax.nn.relu(averaged).astype(jnp.bfloat16)
    return jnp.einsum('cij,cp->ijp', activated.astype(jnp.float32), embed_weight.astype(jnp.float32)).astype(jnp.bfloat16)
```

```python
import jax
import jax.numpy as jnp
from jax import lax
from jax.sharding import PartitionSpec as P

EPSILON = 1e-05


def channel_norm(values, gain_vector):
    centre = values - jnp.mean(values, axis=1, keepdims=True)
    spread = jnp.mean(centre * centre, axis=1, keepdims=True)
    return centre * lax.rsqrt(spread + EPSILON) * gain_vector[None, :, None, None]


def linear_map(values, weight):
    return jnp.einsum("tcrl,ce->terl", values, weight, preferred_element_type=jnp.float32)


def local(
    template_pair,
    pair_mask,
    template_mask,
    in_gain,
    proj_weight,
    gate_weight,
    mid_gain,
    out_weight,
    trans_gain,
    up_weight,
    down_weight,
    final_gain,
    embed_weight,
):
    channels = template_pair.shape[1]
    own_rows = template_pair.shape[2]
    pair_wide = template_pair.astype(jnp.float32)
    normed = channel_norm(pair_wide, in_gain).astype(jnp.bfloat16)
    projected = linear_map(normed, proj_weight)
    pair_weight = pair_mask.astype(jnp.float32)[None, None]
    left_side = (
        jax.nn.sigmoid(projected[:, channels : 2 * channels])
        * projected[:, :channels]
        * pair_weight
    ).astype(jnp.bfloat16)
    right_side = (
        jax.nn.sigmoid(projected[:, 3 * channels :])
        * projected[:, 2 * channels : 3 * channels]
        * pair_weight
    ).astype(jnp.bfloat16)
    gate_value = jax.nn.sigmoid(linear_map(normed, gate_weight))
    both = jnp.stack([left_side, right_side]).reshape(2, 2, channels, own_rows, 2, -1)
    both = both.transpose(1, 2, 4, 0, 3, 5).reshape(256, 2, own_rows, -1)
    moved = lax.all_to_all(both, ("row", "col"), split_axis=0, concat_axis=0, tiled=True)
    moved = moved.transpose(1, 0, 2, 3).reshape(2, 256 * own_rows, -1)
    left_moved, right_moved = moved[0], moved[1]
    core = lax.rem(lax.axis_index("col"), 2)
    half = right_moved.shape[0] // 2
    kept, given = (
        jnp.einsum(
            "ik,jk->ij",
            left_moved,
            lax.dynamic_slice_in_dim(right_moved, which * half, half, 0),
            preferred_element_type=jnp.float32,
        )
        for which in (core, 1 - core)
    )
    swap = [(device, device ^ 1) for device in range(256)]
    taken = lax.ppermute(given, ("row", "col"), swap)
    triangle = (kept + taken).astype(jnp.bfloat16).reshape(256, own_rows, half)
    returned = lax.all_to_all(triangle, ("row", "col"), split_axis=0, concat_axis=0, tiled=True)
    returned = returned.reshape(2, channels, 2, own_rows, half).transpose(0, 1, 3, 2, 4)
    returned = returned.reshape(2, channels, own_rows, 2 * half)
    tri_normed = channel_norm(returned.astype(jnp.float32), mid_gain).astype(jnp.bfloat16)
    updated = pair_wide + gate_value * linear_map(tri_normed, out_weight)
    trans_in = channel_norm(updated, trans_gain).astype(jnp.bfloat16)
    hidden = jax.nn.relu(linear_map(trans_in, up_weight)).astype(jnp.bfloat16)
    stacked = updated + linear_map(hidden, down_weight)
    final = channel_norm(stacked, final_gain)
    mask_values = template_mask.astype(jnp.float32)
    first_row = (lax.axis_index("row") * lax.axis_size("col") + lax.axis_index("col")) * own_rows
    own_mask = lax.dynamic_slice_in_dim(mask_values, first_row, own_rows, 1)
    coverage = own_mask[:, :, None] * mask_values[:, None, :]
    counted = jnp.maximum(jnp.sum(coverage, axis=0), 1.0)
    averaged = jnp.sum(coverage[:, None] * final, axis=0) / counted[None]
    activated = jax.nn.relu(averaged).astype(jnp.bfloat16)
    return jnp.einsum(
        "crl,cp->rlp", activated, embed_weight, preferred_element_type=jnp.float32
    ).astype(jnp.bfloat16)


def solution(mesh):
    return jax.shard_map(
        local,
        mesh=mesh,
        in_specs=(
            P(None, None, ("row", "col"), None),
            P(("row", "col"), None),
            P(),
            P(),
            P(),
            P(),
            P(),
            P(),
            P(),
            P(),
            P(),
            P(),
            P(),
        ),
        out_specs=P(("row", "col"), None, None),
        check_vma=False,
    )
```

```python
import functools

import jax
import jax.numpy as jnp
from jax import lax
from jax.experimental import pallas as pl
from jax.experimental.pallas import tpu as pltpu
from jax.sharding import PartitionSpec as P

EPSILON = 1e-05
MESH = pl.DeviceIdType.MESH
F32, BF16 = jnp.float32, jnp.bfloat16
Z = 8
ROWS = 5
L = 1280
LANES = 256
BLOCKS = L // LANES


def device_at(plane, z, core):
    x, y = plane // 4, lax.rem(plane, 4)
    return ((y // 2) * Z + lax.rem(z + Z, Z), x * 4 + lax.rem(y, 2) * 2 + core)


def column(row_vector):
    n = row_vector.shape[1]
    rows = lax.broadcasted_iota(jnp.int32, (n, n), 0)
    lanes = lax.broadcasted_iota(jnp.int32, (n, n), 1)
    return jnp.sum(jnp.where(rows == lanes, row_vector, 0.0), axis=1, keepdims=True)


def norm(values, gain):
    centre = values - jnp.mean(values, axis=0, keepdims=True)
    spread = jnp.mean(centre * centre, axis=0, keepdims=True)
    return centre * lax.rsqrt(spread + EPSILON) * gain


def dot(a, b):
    return jnp.dot(a, b, preferred_element_type=F32)


def weave(first, second):
    pieces = []
    for g in range(first.shape[0] // 8):
        pieces += [first[8 * g : 8 * g + 8], second[8 * g : 8 * g + 8]]
    return jnp.concatenate(pieces, axis=0)


def unweave(both):
    blocks = both.shape[0] // 8
    return tuple(
        jnp.concatenate([both[8 * b : 8 * b + 8] for b in range(t, blocks, 2)], axis=0)
        for t in range(2)
    )


def whole(ref, sem):
    pltpu.make_async_copy(ref, ref, sem).wait()


def kernel(
    pair,
    pair_mask,
    template_mask,
    in_gain,
    proj_weight,
    gate_weight,
    mid_gain,
    out_weight,
    trans_gain,
    up_weight,
    down_weight,
    final_gain,
    embed_weight,
    result,
    proj_t,
    out_t,
    up_t,
    down_t,
    gains,
    own_mask,
    forth,
    back,
    gate,
    left_sent,
    right_sent,
    left_mid,
    right_mid,
    left_turned,
    right_turned,
    left_held,
    right_held,
    left_flat,
    right_flat,
    right_rows,
    tri_made,
    tri_mid,
    tri_turned,
    tri_held,
    out_held,
    z_left,
    z_right,
    z_tri,
    p_left,
    p_right,
    p_tri,
    across,
    z_out,
    p_out,
    across_out,
    result_sem,
):
    row, col = lax.axis_index("row"), lax.axis_index("col")
    z, core = lax.rem(row, Z), lax.rem(col, 2)
    place = (col // 4) * 4 + (row // Z) * 2 + lax.rem(col // 2, 2)
    device = row * 16 + col
    group = lax.rem(z - core + Z, Z)
    partner = device_at(place, z + 1 - 2 * core, 1 - core)

    barrier = pltpu.get_barrier_semaphore()
    for step in range(1, Z):
        for other in range(2):
            pl.semaphore_signal(
                barrier, inc=1, device_id=device_at(place, z + step, other), device_id_type=MESH
            )
    pl.semaphore_signal(
        barrier, inc=1, device_id=device_at(place, z, 1 - core), device_id_type=MESH
    )

    def greet(step, carry):
        pl.semaphore_signal(
            barrier,
            inc=1,
            device_id=device_at(lax.bitwise_xor(place, step), z, core),
            device_id_type=MESH,
        )
        return carry

    lax.fori_loop(1, 16, greet, 0)

    proj_t[0:256, :] = jnp.transpose(proj_weight[...].astype(F32)).astype(BF16)
    proj_t[256:320, :] = jnp.transpose(gate_weight[...].astype(F32)).astype(BF16)
    out_t[...] = jnp.transpose(out_weight[...].astype(F32)).astype(BF16)
    up_t[...] = jnp.transpose(up_weight[...].astype(F32)).astype(BF16)
    down_t[...] = jnp.transpose(down_weight[...].astype(F32)).astype(BF16)
    for n, vector in enumerate((in_gain, mid_gain, trans_gain, final_gain)):
        gains[n] = column(vector[...])
    lanes = lax.broadcasted_iota(jnp.int32, (2, L), 1)
    for r in range(ROWS):
        own_mask[r] = jnp.sum(
            jnp.where(lanes == device * ROWS + r, template_mask[...].astype(F32), 0.0),
            axis=1,
            keepdims=True,
        )
    at = lax.broadcasted_iota(jnp.int32, (128, 128), 0)
    of = lax.broadcasted_iota(jnp.int32, (128, 128), 1)
    forth[...] = jnp.where(of == (at % 8) * 16 + at // 8, 1.0, 0.0).astype(BF16)
    back[...] = jnp.where(of == (at % 16) * 8 + at // 16, 1.0, 0.0).astype(BF16)

    def make(r):
        for block in range(BLOCKS):
            span = pl.ds(block * LANES, LANES)
            mask = pair_mask[pl.ds(r, 1), span].astype(F32)
            lefts, rights, gates = [], [], []
            for t in range(2):
                normed = norm(pair[t, r, :, span].astype(F32), gains[0]).astype(BF16)
                projected = dot(proj_t[...], normed)
                lefts.append(jax.nn.sigmoid(projected[64:128]) * projected[0:64] * mask)
                rights.append(jax.nn.sigmoid(projected[192:256]) * projected[128:192] * mask)
                gates.append(jax.nn.sigmoid(projected[256:320]))
            right_sent[r, :, span] = weave(*rights).astype(BF16)
            left_sent[r, :, span] = weave(*lefts).astype(BF16)
            gate[r, 0, :, span] = gates[0]
            gate[r, 1, :, span] = gates[1]

    def send_z(r, sent, mid, recv):
        def send(g, slot, where):
            pltpu.make_async_remote_copy(
                sent.at[r, pl.ds(pl.multiple_of(g * 16, 16), 16)],
                mid.at[r, pl.ds(pl.multiple_of(slot * 16, 16), 16)],
                z_out,
                recv.at[r],
                device_id=where,
                device_id_type=MESH,
            ).start()

        for m in (3, 2, 1):
            send(lax.rem(z + m, Z), (3 - m) * 2 + core, device_at(place, z + m, 0))
            send(lax.rem(z + 7 - m, Z), m * 2 + core, device_at(place, z - m, 1))
        send(lax.rem(z + 7 + core, Z), 6 * core + core, device_at(place, z, 1 - core))
        pltpu.make_async_copy(
            sent.at[r, pl.ds(pl.multiple_of(group * 16, 16), 16)],
            mid.at[r, pl.ds(pl.multiple_of((6 - 5 * core) * 16, 16), 16)],
            recv.at[r],
        ).start()

    def send_plane(r, turned, held, recv):
        def send(step, carry):
            other = lax.bitwise_xor(place, step)
            pltpu.make_async_remote_copy(
                turned.at[r, other],
                held.at[r, place],
                p_out,
                recv.at[r],
                device_id=device_at(other, z, core),
                device_id_type=MESH,
            ).start()
            return carry

        lax.fori_loop(1, 16, send, 0)
        pltpu.make_async_copy(turned.at[r, place], held.at[r, place], recv.at[r]).start()

    def turn(r, mid, turned):
        for block in range(BLOCKS):
            span = pl.ds(block * LANES, LANES)
            moved = dot(forth[...], mid[r, :, span])
            turned[r, :, :, span] = moved.reshape(16, 8, LANES).astype(BF16)

    def turn_back(r):
        for block in range(BLOCKS):
            span = pl.ds(block * LANES, LANES)
            value = tri_mid[r, :, :, span].astype(F32).reshape(128, LANES).astype(BF16)
            tri_turned[r, :, span] = dot(back[...], value).astype(BF16)

    def send_back(r):
        def send(slot, where):
            pltpu.make_async_remote_copy(
                tri_turned.at[r, pl.ds(pl.multiple_of(slot * 16, 16), 16)],
                tri_held.at[r, pl.ds(pl.multiple_of(group * 16, 16), 16)],
                z_out,
                z_tri.at[r],
                device_id=where,
                device_id_type=MESH,
            ).start()

        for m in (3, 2, 1):
            for other in range(2):
                slot = ((3 - m) + core * (2 * m - 3)) * 2 + other
                send(slot, device_at(place, z - m + 2 * m * core, other))
        send(7 - 7 * core, device_at(place, z, 1 - core))
        pltpu.make_async_copy(
            tri_turned.at[r, pl.ds(pl.multiple_of((6 - 5 * core) * 16, 16), 16)],
            tri_held.at[r, pl.ds(pl.multiple_of(group * 16, 16), 16)],
            z_tri.at[r],
        ).start()

    def exchange(r):
        return pltpu.make_async_remote_copy(
            right_held.at[core, r],
            right_held.at[core, r],
            across_out,
            across.at[r],
            device_id=partner,
            device_id_type=MESH,
        )

    def send_right(r, carry):
        make(r)

        @pl.when(r == 0)
        def _():
            pl.semaphore_wait(barrier, 30)

        send_z(r, right_sent, right_mid, z_right)
        return carry

    def pass_right(r, carry):
        send_z(r, left_sent, left_mid, z_left)
        whole(right_mid.at[r], z_right.at[r])
        turn(r, right_mid, right_turned)
        send_plane(r, right_turned, right_held.at[core], p_right)
        return carry

    def give_right(r, carry):
        whole(right_held.at[core, r], p_right.at[r])
        exchange(r).start()
        return carry

    def pass_left(r, carry):
        whole(left_mid.at[r], z_left.at[r])
        turn(r, left_mid, left_turned)
        send_plane(r, left_turned, left_held, p_left)
        return carry

    def flatten(r, carry):
        whole(right_held.at[1 - core, r], across.at[r])
        for side in range(2):
            for block in range(BLOCKS):
                span = pl.ds(block * LANES, LANES)
                value = right_held[side, r, :, :, span].astype(F32).reshape(128, LANES)
                start = pl.multiple_of((side * ROWS + r) * 128, 128)
                right_flat[pl.ds(start, 128), span] = value.astype(BF16)
        return carry

    def order(block, carry):
        held = lax.broadcasted_iota(jnp.int32, (1, L), 1)
        chunk = held >> 7
        side = jnp.where(chunk >= ROWS, 1, 0)
        r = chunk - ROWS * side
        source = (held >> 3) & 15
        source_z = (group + 5 + ((held >> 1) & 3) + 4 * side) & 7
        x, y = source >> 2, source & 3
        owner = (((y >> 1) * Z + source_z) * 4 + x) * 4 + (y & 1) * 2 + (held & 1)
        natural = owner * ROWS + r
        start = pl.multiple_of(block * LANES, LANES)
        rows = lax.broadcasted_iota(jnp.int32, (LANES, L), 0) + start
        chosen = jnp.where(rows == natural, 1.0, 0.0).astype(BF16)
        for part in range(BLOCKS):
            span = pl.ds(part * LANES, LANES)
            right_rows[pl.ds(start, LANES), span] = dot(chosen, right_flat[:, span]).astype(BF16)
        return carry

    def multiply(r, carry):
        whole(left_held.at[r], p_left.at[r])
        for block in range(BLOCKS):
            span = pl.ds(block * LANES, LANES)
            value = left_held[r, :, :, span].astype(F32).reshape(128, LANES)
            left_flat[:, span] = value.astype(BF16)
        for block in range(BLOCKS):
            span = pl.ds(block * LANES, LANES)
            product = lax.dot_general(
                left_flat[...],
                right_rows[span, :],
                (((1,), (1,)), ((), ())),
                preferred_element_type=F32,
            )
            tri_made[r, :, :, span] = product.reshape(16, 8, LANES).astype(BF16)
        send_plane(r, tri_made, tri_mid, p_tri)
        return carry

    def give_back(r, carry):
        whole(tri_mid.at[r], p_tri.at[r])
        turn_back(r)
        send_back(r)
        return carry

    def finish(r, carry):
        whole(tri_held.at[r], z_tri.at[r])
        for block in range(BLOCKS):
            span = pl.ds(block * LANES, LANES)
            triangles = unweave(tri_held[r, :, span].astype(F32))
            total, counted = 0.0, 0.0
            for t in range(2):
                tri_normed = norm(triangles[t], gains[1]).astype(BF16)
                updated = pair[t, r, :, span].astype(F32) + gate[r, t, :, span] * dot(
                    out_t[...], tri_normed
                )
                trans_in = norm(updated, gains[2]).astype(BF16)
                hidden = jnp.maximum(dot(up_t[...], trans_in), 0.0).astype(BF16)
                stacked = updated + dot(down_t[...], hidden)
                final = norm(stacked, gains[3])
                coverage = own_mask[r, t : t + 1, :] * template_mask[t : t + 1, span].astype(F32)
                total = total + coverage * final
                counted = counted + coverage
            averaged = total / jnp.maximum(counted, 1.0)
            activated = jnp.transpose(jnp.maximum(averaged, 0.0)).astype(BF16)
            out_held[r, span, :] = dot(activated, embed_weight[...]).astype(BF16)
        pltpu.make_async_copy(out_held.at[r], result.at[r], result_sem.at[r]).start()
        return carry

    lax.fori_loop(0, ROWS, send_right, 0)

    def right_step(r, carry):
        pass_right(r, 0)

        @pl.when(r > 0)
        def _():
            give_right(r - 1, 0)

        return carry

    lax.fori_loop(0, ROWS, right_step, 0)
    give_right(ROWS - 1, 0)
    pass_left(0, 0)
    lax.fori_loop(0, ROWS, flatten, 0)
    lax.fori_loop(0, BLOCKS, order, 0)

    def step(s, carry):
        @pl.when(s < ROWS)
        def _():
            pass_left(s, 0)

        multiply(s - 1, 0)

        @pl.when(s > 1)
        def _():
            give_back(s - 2, 0)

        return carry

    lax.fori_loop(1, ROWS + 1, step, 0)
    give_back(ROWS - 1, 0)
    lax.fori_loop(0, ROWS, finish, 0)

    def left_by_now(r, carry):
        for sent in (left_sent, right_sent, tri_turned):
            whole(sent.at[r, pl.ds(0, 112)], z_out)
        for turned in (left_turned, right_turned, tri_made):
            whole(turned.at[r, pl.ds(0, 15)], p_out)
        whole(right_held.at[core, r], across_out)
        pltpu.make_async_copy(out_held.at[r], result.at[r], result_sem.at[r]).wait()
        return carry

    lax.fori_loop(0, ROWS, left_by_now, 0)


def local(template_pair, pair_mask, template_mask, in_gain, proj_weight, gate_weight, mid_gain,
          out_weight, trans_gain, up_weight, down_weight, final_gain, embed_weight):
    flat = (ROWS, 128, L)
    blocks = (ROWS, 16, 8, L)
    dma = pltpu.SemaphoreType.DMA
    vmem = pltpu.VMEM
    return pl.pallas_call(
        kernel,
        out_shape=jax.ShapeDtypeStruct((ROWS, L, 128), BF16),
        in_specs=[pl.BlockSpec(memory_space=pltpu.VMEM)] * 13,
        out_specs=pl.BlockSpec(memory_space=pl.ANY),
        scratch_shapes=[
            vmem((320, 64), BF16),
            vmem((64, 64), BF16),
            vmem((128, 64), BF16),
            vmem((64, 128), BF16),
            vmem((4, 64, 1), F32),
            vmem((ROWS, 2, 1), F32),
            vmem((128, 128), BF16),
            vmem((128, 128), BF16),
            vmem((ROWS, 2, 64, L), F32),
            vmem(flat, BF16),
            vmem(flat, BF16),
            vmem(flat, BF16),
            vmem(flat, BF16),
            vmem(blocks, BF16),
            vmem(blocks, BF16),
            vmem(blocks, BF16),
            vmem((2, *blocks), BF16),
            vmem((128, L), BF16),
            vmem((L, L), BF16),
            vmem((L, L), BF16),
            vmem(blocks, BF16),
            vmem(blocks, BF16),
            vmem(flat, BF16),
            vmem(flat, BF16),
            vmem((ROWS, L, 128), BF16),
            *[dma((ROWS,)) for _ in range(7)],
            dma,
            dma,
            dma,
            dma((ROWS,)),
        ],
        compiler_params=pltpu.CompilerParams(
            collective_id=0, has_side_effects=True, vmem_limit_bytes=60 * 2**20
        ),
    )(
        template_pair.transpose(0, 2, 1, 3),
        pair_mask,
        template_mask,
        in_gain.reshape(1, -1),
        proj_weight,
        gate_weight,
        mid_gain.reshape(1, -1),
        out_weight,
        trans_gain.reshape(1, -1),
        up_weight,
        down_weight,
        final_gain.reshape(1, -1),
        embed_weight,
    )


def solution(mesh):
    return jax.shard_map(
        local,
        mesh=mesh,
        in_specs=(P(None, None, ("row", "col"), None), P(("row", "col"), None), *[P()] * 11),
        out_specs=P(("row", "col"), None, None),
        check_vma=False,
    )
```

```python
import functools

import jax
import jax.numpy as jnp
from jax import lax
from jax.experimental import pallas as pl
from jax.experimental.pallas import tpu as pltpu
from jax.sharding import PartitionSpec as P

EPSILON = 1e-05
MESH = pl.DeviceIdType.MESH
F32, BF16 = jnp.float32, jnp.bfloat16
Z = 8
ROWS = 5
L = 1280
LANES = 256
BLOCKS = L // LANES
AHEAD = 2


def device_at(plane, z, core):
    row = ((plane & 2) << 2) + (z & (Z - 1))
    return (row, (plane & 12) + ((plane & 1) << 1) + core)


def column(row_vector):
    n = row_vector.shape[1]
    rows = lax.broadcasted_iota(jnp.int32, (n, n), 0)
    lanes = lax.broadcasted_iota(jnp.int32, (n, n), 1)
    return jnp.sum(jnp.where(rows == lanes, row_vector, 0.0), axis=1, keepdims=True)


def norm(values, gain):
    centre = values - jnp.mean(values, axis=-2, keepdims=True)
    spread = jnp.mean(centre * centre, axis=-2, keepdims=True)
    return centre * lax.rsqrt(spread + EPSILON) * gain


def norm_both(values, gain):
    return norm(values.reshape(2, 64, -1), gain).reshape(values.shape)


def dot(a, b):
    return jnp.dot(a, b, preferred_element_type=F32)


def weave(first, second):
    pieces = []
    for g in range(first.shape[0] // 8):
        pieces += [first[8 * g : 8 * g + 8], second[8 * g : 8 * g + 8]]
    return jnp.concatenate(pieces, axis=0)


def unweave(both):
    blocks = both.shape[0] // 8
    pieces = [both[8 * b : 8 * b + 8] for t in range(2) for b in range(t, blocks, 2)]
    return jnp.concatenate(pieces, axis=0)


def whole(ref, sem):
    pltpu.make_async_copy(ref, ref, sem).wait()


def kernel(
    pair,
    pair_mask,
    template_mask,
    in_gain,
    proj_weight,
    gate_weight,
    mid_gain,
    out_weight,
    trans_gain,
    up_weight,
    down_weight,
    final_gain,
    result,
    proj_t,
    out_t,
    up_t,
    down_t,
    gains,
    own_mask,
    forth,
    back,
    gate,
    left_sent,
    right_sent,
    left_mid,
    right_mid,
    left_turned,
    right_turned,
    left_held,
    right_held,
    left_flat,
    tri_flat,
    right_flat,
    right_rows,
    tri_made,
    tri_mid,
    tri_turned,
    tri_held,
    out_held,
    z_left,
    z_right,
    z_tri,
    p_left,
    p_right,
    p_tri,
    across,
    z_out,
    p_out,
    across_out,
    result_sem,
):
    row, col = lax.axis_index("row"), lax.axis_index("col")
    z, core = row & (Z - 1), col & 1
    place = (col & 12) + ((row & Z) >> 2) + ((col & 2) >> 1)
    device = row * 16 + col
    group = (z - core) & (Z - 1)
    partner = device_at(place, z + 1 - 2 * core, 1 - core)

    barrier = pltpu.get_barrier_semaphore()
    for step in range(1, Z):
        for other in range(2):
            pl.semaphore_signal(
                barrier, inc=1, device_id=device_at(place, z + step, other), device_id_type=MESH
            )
    pl.semaphore_signal(
        barrier, inc=1, device_id=device_at(place, z, 1 - core), device_id_type=MESH
    )

    def greet(step, carry):
        pl.semaphore_signal(
            barrier,
            inc=1,
            device_id=device_at(lax.bitwise_xor(place, step), z, core),
            device_id_type=MESH,
        )
        return carry

    lax.fori_loop(1, 16, greet, 0)

    proj_t[0:256, :] = jnp.transpose(proj_weight[...].astype(F32)).astype(BF16)
    proj_t[256:320, :] = jnp.transpose(gate_weight[...].astype(F32)).astype(BF16)
    out_t[...] = jnp.zeros_like(out_t)
    up_t[...] = jnp.zeros_like(up_t)
    down_t[...] = jnp.zeros_like(down_t)
    for t in range(2):
        own, wide = pl.ds(64 * t, 64), pl.ds(128 * t, 128)
        out_t[own, own] = jnp.transpose(out_weight[...].astype(F32)).astype(BF16)
        up_t[wide, own] = jnp.transpose(up_weight[...].astype(F32)).astype(BF16)
        down_t[own, wide] = down_weight[...]
    for n, vector in enumerate((in_gain, mid_gain, trans_gain, final_gain)):
        gains[n] = column(vector[...])
    lanes = lax.broadcasted_iota(jnp.int32, (2, L), 1)
    for r in range(ROWS):
        own_mask[r] = jnp.sum(
            jnp.where(lanes == device * ROWS + r, template_mask[...].astype(F32), 0.0),
            axis=1,
            keepdims=True,
        )
    at = lax.broadcasted_iota(jnp.int32, (128, 128), 0)
    of = lax.broadcasted_iota(jnp.int32, (128, 128), 1)
    forth[...] = jnp.where(of == (at % 8) * 16 + at // 8, 1.0, 0.0).astype(BF16)
    back[...] = jnp.where(of == (at % 16) * 8 + at // 16, 1.0, 0.0).astype(BF16)

    def make(r):
        for block in range(BLOCKS):
            span = pl.ds(block * LANES, LANES)
            mask = pair_mask[pl.ds(r, 1), span].astype(F32)
            lefts, rights, gates = [], [], []
            for t in range(2):
                normed = norm(pair[t, r, :, span].astype(F32), gains[0]).astype(BF16)
                projected = dot(proj_t[...], normed)
                lefts.append(jax.nn.sigmoid(projected[64:128]) * projected[0:64] * mask)
                rights.append(jax.nn.sigmoid(projected[192:256]) * projected[128:192] * mask)
                gates.append(jax.nn.sigmoid(projected[256:320]))
            right_sent[r, :, span] = weave(*rights).astype(BF16)
            left_sent[r, :, span] = weave(*lefts).astype(BF16)
            gate[r, :, span] = jnp.concatenate(gates, axis=0)

    def send_z(r, sent, mid, recv):
        def send(g, slot, where):
            pltpu.make_async_remote_copy(
                sent.at[r, pl.ds(pl.multiple_of(g * 16, 16), 16)],
                mid.at[r, pl.ds(pl.multiple_of(slot * 16, 16), 16)],
                z_out,
                recv.at[r],
                device_id=where,
                device_id_type=MESH,
            ).start()

        for m in (3, 2, 1):
            send((z + m) & (Z - 1), (3 - m) * 2 + core, device_at(place, z + m, 0))
            send((z + 7 - m) & (Z - 1), m * 2 + core, device_at(place, z - m, 1))
        send((z + 7 + core) & (Z - 1), 6 * core + core, device_at(place, z, 1 - core))
        pltpu.make_async_copy(
            sent.at[r, pl.ds(pl.multiple_of(group * 16, 16), 16)],
            mid.at[r, pl.ds(pl.multiple_of((6 - 5 * core) * 16, 16), 16)],
            recv.at[r],
        ).start()

    def send_plane(r, turned, held, recv):
        def send(step, carry):
            other = lax.bitwise_xor(place, step)
            pltpu.make_async_remote_copy(
                turned.at[r, other],
                held.at[r, place],
                p_out,
                recv.at[r],
                device_id=device_at(other, z, core),
                device_id_type=MESH,
            ).start()
            return carry

        lax.fori_loop(1, 16, send, 0)
        pltpu.make_async_copy(turned.at[r, place], held.at[r, place], recv.at[r]).start()

    def turn(r, mid, turned):
        for block in range(BLOCKS):
            span = pl.ds(block * LANES, LANES)
            moved = dot(forth[...], mid[r, :, span])
            turned[r, :, :, span] = moved.reshape(16, 8, LANES).astype(BF16)

    def turn_back(r):
        for block in range(BLOCKS):
            span = pl.ds(block * LANES, LANES)
            value = tri_mid[r, :, :, span].astype(F32).reshape(128, LANES).astype(BF16)
            tri_turned[r, :, span] = dot(back[...], value).astype(BF16)

    def send_back(r):
        def send(slot, where):
            pltpu.make_async_remote_copy(
                tri_turned.at[r, pl.ds(pl.multiple_of(slot * 16, 16), 16)],
                tri_held.at[r, pl.ds(pl.multiple_of(group * 16, 16), 16)],
                z_out,
                z_tri.at[r],
                device_id=where,
                device_id_type=MESH,
            ).start()

        for m in (3, 2, 1):
            for other in range(2):
                slot = ((3 - m) + core * (2 * m - 3)) * 2 + other
                send(slot, device_at(place, z - m + 2 * m * core, other))
        send(7 - 7 * core, device_at(place, z, 1 - core))
        pltpu.make_async_copy(
            tri_turned.at[r, pl.ds(pl.multiple_of((6 - 5 * core) * 16, 16), 16)],
            tri_held.at[r, pl.ds(pl.multiple_of(group * 16, 16), 16)],
            z_tri.at[r],
        ).start()

    def exchange(r):
        return pltpu.make_async_remote_copy(
            right_held.at[core, r],
            right_held.at[core, r],
            across_out,
            across.at[r],
            device_id=partner,
            device_id_type=MESH,
        )

    def send_right(r, carry):
        make(r)

        @pl.when(r == 0)
        def _():
            pl.semaphore_wait(barrier, 30)

        send_z(r, right_sent, right_mid, z_right)
        return carry

    def pass_right(r, carry):
        whole(right_mid.at[r], z_right.at[r])
        turn(r, right_mid, right_turned)
        send_plane(r, right_turned, right_held.at[core], p_right)
        return carry

    def give_right(r, carry):
        whole(right_held.at[core, r], p_right.at[r])
        exchange(r).start()
        return carry

    def pass_left(r, carry):
        whole(left_mid.at[r], z_left.at[r])
        turn(r, left_mid, left_turned)
        send_plane(r, left_turned, left_held, p_left)
        return carry

    def flatten(r, carry):
        whole(right_held.at[1 - core, r], across.at[r])
        for side in range(2):
            for block in range(BLOCKS):
                span = pl.ds(block * LANES, LANES)
                value = right_held[side, r, :, :, span].astype(F32).reshape(128, LANES)
                start = pl.multiple_of((side * ROWS + r) * 128, 128)
                right_flat[pl.ds(start, 128), span] = value.astype(BF16)
        return carry

    def order(block, carry):
        held = lax.broadcasted_iota(jnp.int32, (1, L), 1)
        chunk = held >> 7
        side = jnp.where(chunk >= ROWS, 1, 0)
        r = chunk - ROWS * side
        source = (held >> 3) & 15
        source_z = (group + 5 + ((held >> 1) & 3) + 4 * side) & 7
        x, y = source >> 2, source & 3
        owner = (((y >> 1) * Z + source_z) * 4 + x) * 4 + (y & 1) * 2 + (held & 1)
        natural = owner * ROWS + r
        start = pl.multiple_of(block * LANES, LANES)
        rows = lax.broadcasted_iota(jnp.int32, (LANES, L), 0) + start
        right_rows[pl.ds(start, LANES), :] = jnp.where(rows == natural, 1.0, 0.0).astype(BF16)
        return carry

    def multiply(r, carry):
        whole(left_held.at[r], p_left.at[r])
        for block in range(BLOCKS):
            span = pl.ds(block * LANES, LANES)
            value = left_held[r, :, :, span].astype(F32).reshape(128, LANES)
            left_flat[:, span] = value.astype(BF16)
        for block in range(BLOCKS):
            span = pl.ds(block * LANES, LANES)
            product = lax.dot_general(
                left_flat[...],
                right_flat[span, :],
                (((1,), (1,)), ((), ())),
                preferred_element_type=F32,
            )
            tri_flat[:, span] = product.astype(BF16)
        for block in range(BLOCKS):
            span = pl.ds(block * LANES, LANES)
            moved = lax.dot_general(
                tri_flat[...],
                right_rows[span, :],
                (((1,), (1,)), ((), ())),
                preferred_element_type=F32,
            )
            tri_made[r, :, :, span] = moved.reshape(16, 8, LANES).astype(BF16)
        send_plane(r, tri_made, tri_mid, p_tri)
        return carry

    def give_back(r, carry):
        whole(tri_mid.at[r], p_tri.at[r])
        turn_back(r)
        send_back(r)
        return carry

    def finish(r, carry):
        whole(tri_held.at[r], z_tri.at[r])
        for block in range(BLOCKS):
            span = pl.ds(block * LANES, LANES)
            triangle = unweave(tri_held[r, :, span].astype(F32))
            pairs = jnp.concatenate([pair[t, r, :, span].astype(F32) for t in range(2)], axis=0)
            tri_normed = norm_both(triangle, gains[1]).astype(BF16)
            updated = pairs + gate[r, :, span] * dot(out_t[...], tri_normed)
            trans_in = norm_both(updated, gains[2]).astype(BF16)
            hidden = jnp.maximum(dot(up_t[...], trans_in), 0.0).astype(BF16)
            final = norm_both(updated + dot(down_t[...], hidden), gains[3])
            coverage = own_mask[r] * template_mask[:, span].astype(F32)
            total = coverage[0:1] * final[0:64] + coverage[1:2] * final[64:128]
            averaged = total / jnp.maximum(coverage[0:1] + coverage[1:2], 1.0)
            out_held[r, :, span] = jnp.maximum(averaged, 0.0).astype(BF16)
        pltpu.make_async_copy(out_held.at[r], result.at[r], result_sem.at[r]).start()
        return carry

    lax.fori_loop(0, ROWS, send_right, 0)

    def send_left(r):
        send_z(r, left_sent, left_mid, z_left)

    def right_step(r, carry):
        pass_right(r, 0)

        @pl.when(r == ROWS - 1)
        def _():
            for first in range(AHEAD):
                send_left(first)

        @pl.when(r > 0)
        def _():
            give_right(r - 1, 0)

        return carry

    lax.fori_loop(0, BLOCKS, order, 0)
    lax.fori_loop(0, ROWS, right_step, 0)
    give_right(ROWS - 1, 0)
    pass_left(0, 0)
    send_left(AHEAD)
    lax.fori_loop(0, ROWS, flatten, 0)

    def step(s, carry):
        pass_left(s, 0)

        @pl.when(s + AHEAD < ROWS)
        def _():
            send_left(s + AHEAD)

        multiply(s - 1, 0)
        return carry

    lax.fori_loop(1, ROWS - 1, step, 0)
    give_back(0, 0)
    pass_left(ROWS - 1, 0)
    give_back(1, 0)
    multiply(ROWS - 2, 0)
    give_back(2, 0)
    multiply(ROWS - 1, 0)
    give_back(3, 0)
    give_back(4, 0)
    lax.fori_loop(0, ROWS, finish, 0)

    def left_by_now(r, carry):
        for sent in (left_sent, right_sent, tri_turned):
            whole(sent.at[r, pl.ds(0, 112)], z_out)
        for turned in (left_turned, right_turned, tri_made):
            whole(turned.at[r, pl.ds(0, 15)], p_out)
        whole(right_held.at[core, r], across_out)
        pltpu.make_async_copy(out_held.at[r], result.at[r], result_sem.at[r]).wait()
        return carry

    lax.fori_loop(0, ROWS, left_by_now, 0)


def local(template_pair, pair_mask, template_mask, in_gain, proj_weight, gate_weight, mid_gain,
          out_weight, trans_gain, up_weight, down_weight, final_gain, embed_weight):
    flat = (ROWS, 128, L)
    blocks = (ROWS, 16, 8, L)
    dma = pltpu.SemaphoreType.DMA
    vmem = pltpu.VMEM
    activated = pl.pallas_call(
        kernel,
        out_shape=jax.ShapeDtypeStruct((ROWS, 64, L), BF16),
        in_specs=[pl.BlockSpec(memory_space=pltpu.VMEM)] * 12,
        out_specs=pl.BlockSpec(memory_space=pl.ANY),
        scratch_shapes=[
            vmem((320, 64), BF16),
            vmem((128, 128), BF16),
            vmem((256, 128), BF16),
            vmem((128, 256), BF16),
            vmem((4, 64, 1), F32),
            vmem((ROWS, 2, 1), F32),
            vmem((128, 128), BF16),
            vmem((128, 128), BF16),
            vmem((ROWS, 128, L), F32),
            vmem(flat, BF16),
            vmem(flat, BF16),
            vmem(flat, BF16),
            vmem(flat, BF16),
            vmem(blocks, BF16),
            vmem(blocks, BF16),
            vmem(blocks, BF16),
            vmem((2, *blocks), BF16),
            vmem((128, L), BF16),
            vmem((128, L), BF16),
            vmem((L, L), BF16),
            vmem((L, L), BF16),
            vmem(blocks, BF16),
            vmem(blocks, BF16),
            vmem(flat, BF16),
            vmem(flat, BF16),
            vmem((ROWS, 64, L), BF16),
            *[dma((ROWS,)) for _ in range(7)],
            dma,
            dma,
            dma,
            dma((ROWS,)),
        ],
        compiler_params=pltpu.CompilerParams(
            collective_id=0, has_side_effects=True, vmem_limit_bytes=60 * 2**20
        ),
    )(
        template_pair.transpose(0, 2, 1, 3),
        pair_mask,
        template_mask,
        in_gain.reshape(1, -1),
        proj_weight,
        gate_weight,
        mid_gain.reshape(1, -1),
        out_weight,
        trans_gain.reshape(1, -1),
        up_weight,
        down_weight.T,
        final_gain.reshape(1, -1),
    )
    return jnp.einsum(
        "rcl,cp->rlp", activated, embed_weight, preferred_element_type=F32
    ).astype(BF16)


def solution(mesh):
    return jax.shard_map(
        local,
        mesh=mesh,
        in_specs=(P(None, None, ("row", "col"), None), P(("row", "col"), None), *[P()] * 11),
        out_specs=P(("row", "col"), None, None),
        check_vma=False,
    )
```

```python
import functools

import jax
import jax.numpy as jnp
from jax import lax
from jax.experimental import pallas as pl
from jax.experimental.pallas import tpu as pltpu
from jax.sharding import PartitionSpec as P

EPSILON = 1e-05
MESH = pl.DeviceIdType.MESH
F32, BF16 = jnp.float32, jnp.bfloat16
Z = 8
ROWS = 5
L = 1280
LANES = 256
BLOCKS = L // LANES
WIDE = 640


def device_at(plane, z, core):
    row = ((plane & 2) << 2) + (z & (Z - 1))
    return (row, (plane & 12) + ((plane & 1) << 1) + core)


def column(row_vector):
    n = row_vector.shape[1]
    rows = lax.broadcasted_iota(jnp.int32, (n, n), 0)
    lanes = lax.broadcasted_iota(jnp.int32, (n, n), 1)
    return jnp.sum(jnp.where(rows == lanes, row_vector, 0.0), axis=1, keepdims=True)


def norm(values, gain):
    centre = values - jnp.mean(values, axis=-2, keepdims=True)
    spread = jnp.mean(centre * centre, axis=-2, keepdims=True)
    return centre * lax.rsqrt(spread + EPSILON) * gain


def norm_both(values, gain):
    return norm(values.reshape(2, 64, -1), gain).reshape(values.shape)


def dot(a, b):
    return jnp.dot(a, b, preferred_element_type=F32)


def weave(first, second):
    pieces = []
    for g in range(first.shape[0] // 8):
        pieces += [first[8 * g : 8 * g + 8], second[8 * g : 8 * g + 8]]
    return jnp.concatenate(pieces, axis=0)


def unweave(both):
    blocks = both.shape[0] // 8
    pieces = [both[8 * b : 8 * b + 8] for t in range(2) for b in range(t, blocks, 2)]
    return jnp.concatenate(pieces, axis=0)


def whole(ref, sem):
    pltpu.make_async_copy(ref, ref, sem).wait()


def kernel(
    pair,
    pair_mask,
    template_mask,
    in_gain,
    proj_weight,
    gate_weight,
    mid_gain,
    out_weight,
    trans_gain,
    up_weight,
    down_weight,
    final_gain,
    result,
    proj_t,
    out_t,
    up_t,
    down_t,
    gains,
    own_mask,
    forth,
    back,
    gate,
    left_sent,
    right_sent,
    left_mid,
    right_mid,
    left_turned,
    right_turned,
    left_held,
    right_held,
    left_flat,
    tri_flat,
    right_flat,
    right_rows,
    tri_made,
    tri_mid,
    tri_turned,
    tri_held,
    out_held,
    z_left,
    z_right,
    z_tri,
    p_left,
    p_right,
    p_tri,
    across,
    z_out,
    p_out,
    across_out,
    result_sem,
):
    row, col = lax.axis_index("row"), lax.axis_index("col")
    z, core = row & (Z - 1), col & 1
    place = (col & 12) + ((row & Z) >> 2) + ((col & 2) >> 1)
    device = row * 16 + col
    group = (z - core) & (Z - 1)
    partner = device_at(place, z + 1 - 2 * core, 1 - core)

    barrier = pltpu.get_barrier_semaphore()
    for step in range(1, Z):
        for other in range(2):
            pl.semaphore_signal(
                barrier, inc=1, device_id=device_at(place, z + step, other), device_id_type=MESH
            )
    pl.semaphore_signal(
        barrier, inc=1, device_id=device_at(place, z, 1 - core), device_id_type=MESH
    )

    def greet(step, carry):
        pl.semaphore_signal(
            barrier,
            inc=1,
            device_id=device_at(lax.bitwise_xor(place, step), z, core),
            device_id_type=MESH,
        )
        return carry

    lax.fori_loop(1, 16, greet, 0)

    proj_t[0:256, :] = jnp.transpose(proj_weight[...].astype(F32)).astype(BF16)
    proj_t[256:320, :] = jnp.transpose(gate_weight[...].astype(F32)).astype(BF16)
    out_t[...] = jnp.zeros_like(out_t)
    up_t[...] = jnp.zeros_like(up_t)
    down_t[...] = jnp.zeros_like(down_t)
    for t in range(2):
        own, wide = pl.ds(64 * t, 64), pl.ds(128 * t, 128)
        out_t[own, own] = jnp.transpose(out_weight[...].astype(F32)).astype(BF16)
        up_t[wide, own] = jnp.transpose(up_weight[...].astype(F32)).astype(BF16)
        down_t[own, wide] = down_weight[...]
    for n, vector in enumerate((in_gain, mid_gain, trans_gain, final_gain)):
        gains[n] = column(vector[...])
    lanes = lax.broadcasted_iota(jnp.int32, (2, L), 1)
    for r in range(ROWS):
        own_mask[r] = jnp.sum(
            jnp.where(lanes == device * ROWS + r, template_mask[...].astype(F32), 0.0),
            axis=1,
            keepdims=True,
        )
    at = lax.broadcasted_iota(jnp.int32, (128, 128), 0)
    of = lax.broadcasted_iota(jnp.int32, (128, 128), 1)
    forth[...] = jnp.where(of == (at % 8) * 16 + at // 8, 1.0, 0.0).astype(BF16)
    back[...] = jnp.where(of == (at % 16) * 8 + at // 16, 1.0, 0.0).astype(BF16)

    def make(r):
        for block in range(BLOCKS):
            span = pl.ds(block * LANES, LANES)
            mask = pair_mask[pl.ds(r, 1), span].astype(F32)
            lefts, rights, gates = [], [], []
            for t in range(2):
                normed = norm(pair[t, r, :, span].astype(F32), gains[0]).astype(BF16)
                projected = dot(proj_t[...], normed)
                lefts.append(jax.nn.sigmoid(projected[64:128]) * projected[0:64] * mask)
                rights.append(jax.nn.sigmoid(projected[192:256]) * projected[128:192] * mask)
                gates.append(jax.nn.sigmoid(projected[256:320]))
            right_sent[r, :, span] = weave(*rights).astype(BF16)
            left_sent[r, :, span] = weave(*lefts).astype(BF16)
            gate[r, :, span] = jnp.concatenate(gates, axis=0)

    def send_z(r, sent, mid, recv):
        def send(g, slot, where):
            pltpu.make_async_remote_copy(
                sent.at[r, pl.ds(pl.multiple_of(g * 16, 16), 16)],
                mid.at[r, pl.ds(pl.multiple_of(slot * 16, 16), 16)],
                z_out,
                recv.at[r],
                device_id=where,
                device_id_type=MESH,
            ).start()

        for m in (3, 2, 1):
            send((z + m) & (Z - 1), (3 - m) * 2 + core, device_at(place, z + m, 0))
            send((z + 7 - m) & (Z - 1), m * 2 + core, device_at(place, z - m, 1))
        send((z + 7 + core) & (Z - 1), 6 * core + core, device_at(place, z, 1 - core))
        pltpu.make_async_copy(
            sent.at[r, pl.ds(pl.multiple_of(group * 16, 16), 16)],
            mid.at[r, pl.ds(pl.multiple_of((6 - 5 * core) * 16, 16), 16)],
            recv.at[r],
        ).start()

    def send_plane(r, turned, held, recv):
        def send(step, carry):
            other = lax.bitwise_xor(place, step)
            pltpu.make_async_remote_copy(
                turned.at[r, other],
                held.at[r, place],
                p_out,
                recv.at[r],
                device_id=device_at(other, z, core),
                device_id_type=MESH,
            ).start()
            return carry

        lax.fori_loop(1, 16, send, 0)
        pltpu.make_async_copy(turned.at[r, place], held.at[r, place], recv.at[r]).start()

    def turn(r, mid, turned):
        for block in range(BLOCKS):
            span = pl.ds(block * LANES, LANES)
            moved = dot(forth[...], mid[r, :, span])
            turned[r, :, :, span] = moved.reshape(16, 8, LANES).astype(BF16)

    def turn_back(r):
        for block in range(BLOCKS):
            span = pl.ds(block * LANES, LANES)
            value = tri_mid[r, :, :, span].astype(F32).reshape(128, LANES).astype(BF16)
            tri_turned[r, :, span] = dot(back[...], value).astype(BF16)

    def send_back(r):
        def send(slot, where):
            pltpu.make_async_remote_copy(
                tri_turned.at[r, pl.ds(pl.multiple_of(slot * 16, 16), 16)],
                tri_held.at[r, pl.ds(pl.multiple_of(group * 16, 16), 16)],
                z_out,
                z_tri.at[r],
                device_id=where,
                device_id_type=MESH,
            ).start()

        for m in (3, 2, 1):
            for other in range(2):
                slot = ((3 - m) + core * (2 * m - 3)) * 2 + other
                send(slot, device_at(place, z - m + 2 * m * core, other))
        send(7 - 7 * core, device_at(place, z, 1 - core))
        pltpu.make_async_copy(
            tri_turned.at[r, pl.ds(pl.multiple_of((6 - 5 * core) * 16, 16), 16)],
            tri_held.at[r, pl.ds(pl.multiple_of(group * 16, 16), 16)],
            z_tri.at[r],
        ).start()

    def exchange(r):
        return pltpu.make_async_remote_copy(
            right_held.at[core, r],
            right_held.at[core, r],
            across_out,
            across.at[r],
            device_id=partner,
            device_id_type=MESH,
        )

    def send_right(r, carry):
        make(r)

        @pl.when(r == 0)
        def _():
            pl.semaphore_wait(barrier, 30)

        send_z(r, right_sent, right_mid, z_right)
        return carry

    def pass_right(r, carry):
        whole(right_mid.at[r], z_right.at[r])
        turn(r, right_mid, right_turned)
        send_plane(r, right_turned, right_held.at[core], p_right)
        return carry

    def give_right(r, carry):
        whole(right_held.at[core, r], p_right.at[r])
        exchange(r).start()
        return carry

    def pass_left(r, carry):
        whole(left_mid.at[r], z_left.at[r])
        turn(r, left_mid, left_turned)
        send_plane(r, left_turned, left_held, p_left)
        return carry

    def flatten(r, carry):
        whole(right_held.at[1 - core, r], across.at[r])
        for side in range(2):
            for block in range(BLOCKS):
                span = pl.ds(block * LANES, LANES)
                value = right_held[side, r, :, :, span].astype(F32).reshape(128, LANES)
                start = pl.multiple_of((side * ROWS + r) * 128, 128)
                right_flat[pl.ds(start, 128), span] = value.astype(BF16)
        return carry

    def order(block, carry):
        held = lax.broadcasted_iota(jnp.int32, (1, L), 1)
        chunk = held >> 7
        side = jnp.where(chunk >= ROWS, 1, 0)
        r = chunk - ROWS * side
        source = (held >> 3) & 15
        source_z = (group + 5 + ((held >> 1) & 3) + 4 * side) & 7
        x, y = source >> 2, source & 3
        owner = (((y >> 1) * Z + source_z) * 4 + x) * 4 + (y & 1) * 2 + (held & 1)
        natural = owner * ROWS + r
        start = pl.multiple_of(block * LANES, LANES)
        rows = lax.broadcasted_iota(jnp.int32, (LANES, L), 0) + start
        right_rows[pl.ds(start, LANES), :] = jnp.where(rows == natural, 1.0, 0.0).astype(BF16)
        return carry

    def multiply(r, carry):
        whole(left_held.at[r], p_left.at[r])
        for block in range(BLOCKS):
            span = pl.ds(block * LANES, LANES)
            value = left_held[r, :, :, span].astype(F32).reshape(128, LANES)
            left_flat[:, span] = value.astype(BF16)
        for block in range(BLOCKS):
            span = pl.ds(block * LANES, LANES)
            product = lax.dot_general(
                left_flat[...],
                right_flat[span, :],
                (((1,), (1,)), ((), ())),
                preferred_element_type=F32,
            )
            tri_flat[:, span] = product.astype(BF16)
        for block in range(BLOCKS):
            span = pl.ds(block * LANES, LANES)
            moved = lax.dot_general(
                tri_flat[...],
                right_rows[span, :],
                (((1,), (1,)), ((), ())),
                preferred_element_type=F32,
            )
            tri_made[r, :, :, span] = moved.reshape(16, 8, LANES).astype(BF16)
        send_plane(r, tri_made, tri_mid, p_tri)
        return carry

    def give_back(r, carry):
        whole(tri_mid.at[r], p_tri.at[r])
        turn_back(r)
        send_back(r)
        return carry

    def finish(r, carry):
        whole(tri_held.at[r], z_tri.at[r])
        for block in range(L // WIDE):
            span = pl.ds(block * WIDE, WIDE)
            triangle = unweave(tri_held[r, :, span].astype(F32))
            pairs = jnp.concatenate([pair[t, r, :, span].astype(F32) for t in range(2)], axis=0)
            tri_normed = norm_both(triangle, gains[1]).astype(BF16)
            updated = pairs + gate[r, :, span] * dot(out_t[...], tri_normed)
            trans_in = norm_both(updated, gains[2]).astype(BF16)
            hidden = jnp.maximum(dot(up_t[...], trans_in), 0.0).astype(BF16)
            final = norm_both(updated + dot(down_t[...], hidden), gains[3])
            coverage = own_mask[r] * template_mask[:, span].astype(F32)
            total = coverage[0:1] * final[0:64] + coverage[1:2] * final[64:128]
            averaged = total / jnp.maximum(coverage[0:1] + coverage[1:2], 1.0)
            out_held[r, :, span] = jnp.maximum(averaged, 0.0).astype(BF16)
        pltpu.make_async_copy(out_held.at[r], result.at[r], result_sem.at[r]).start()
        return carry

    lax.fori_loop(0, ROWS, send_right, 0)

    def send_left(r):
        send_z(r, left_sent, left_mid, z_left)

    def right_step(r, carry):
        pass_right(r, 0)

        @pl.when(r == 4)
        def _():
            for first in [0]:
                send_left(first)

        @pl.when(r > 0)
        def _():
            give_right(r - 1, 0)

        return carry

    lax.fori_loop(0, BLOCKS, order, 0)
    lax.fori_loop(0, ROWS, right_step, 0)
    give_right(ROWS - 1, 0)
    send_left(1)
    pass_left(0, 0)
    send_left(2)
    lax.fori_loop(0, ROWS, flatten, 0)

    def step(s, carry):
        pass_left(s, 0)
        send_left(s + 2)
        multiply(s - 1, 0)
        return carry

    lax.fori_loop(1, ROWS - 2, step, 0)
    pass_left(ROWS - 2, 0)
    give_back(0, 0)
    multiply(ROWS - 3, 0)
    pass_left(ROWS - 1, 0)
    give_back(1, 0)
    multiply(ROWS - 2, 0)
    give_back(2, 0)
    multiply(ROWS - 1, 0)
    give_back(3, 0)
    give_back(4, 0)
    lax.fori_loop(0, ROWS, finish, 0)

    def left_by_now(r, carry):
        for sent in (left_sent, right_sent, tri_turned):
            whole(sent.at[r, pl.ds(0, 112)], z_out)
        for turned in (left_turned, right_turned, tri_made):
            whole(turned.at[r, pl.ds(0, 15)], p_out)
        whole(right_held.at[core, r], across_out)
        pltpu.make_async_copy(out_held.at[r], result.at[r], result_sem.at[r]).wait()
        return carry

    lax.fori_loop(0, ROWS, left_by_now, 0)


def local(template_pair, pair_mask, template_mask, in_gain, proj_weight, gate_weight, mid_gain,
          out_weight, trans_gain, up_weight, down_weight, final_gain, embed_weight):
    flat = (ROWS, 128, L)
    blocks = (ROWS, 16, 8, L)
    dma = pltpu.SemaphoreType.DMA
    vmem = pltpu.VMEM
    activated = pl.pallas_call(
        kernel,
        out_shape=jax.ShapeDtypeStruct((ROWS, 64, L), BF16),
        in_specs=[pl.BlockSpec(memory_space=pltpu.VMEM)] * 12,
        out_specs=pl.BlockSpec(memory_space=pl.ANY),
        scratch_shapes=[
            vmem((320, 64), BF16),
            vmem((128, 128), BF16),
            vmem((256, 128), BF16),
            vmem((128, 256), BF16),
            vmem((4, 64, 1), F32),
            vmem((ROWS, 2, 1), F32),
            vmem((128, 128), BF16),
            vmem((128, 128), BF16),
            vmem((ROWS, 128, L), F32),
            vmem(flat, BF16),
            vmem(flat, BF16),
            vmem(flat, BF16),
            vmem(flat, BF16),
            vmem(blocks, BF16),
            vmem(blocks, BF16),
            vmem(blocks, BF16),
            vmem((2, *blocks), BF16),
            vmem((128, L), BF16),
            vmem((128, L), BF16),
            vmem((L, L), BF16),
            vmem((L, L), BF16),
            vmem(blocks, BF16),
            vmem(blocks, BF16),
            vmem(flat, BF16),
            vmem(flat, BF16),
            vmem((ROWS, 64, L), BF16),
            *[dma((ROWS,)) for _ in range(7)],
            dma,
            dma,
            dma,
            dma((ROWS,)),
        ],
        compiler_params=pltpu.CompilerParams(
            collective_id=0, has_side_effects=True, vmem_limit_bytes=60 * 2**20
        ),
    )(
        template_pair.transpose(0, 2, 1, 3),
        pair_mask,
        template_mask,
        in_gain.reshape(1, -1),
        proj_weight,
        gate_weight,
        mid_gain.reshape(1, -1),
        out_weight,
        trans_gain.reshape(1, -1),
        up_weight,
        down_weight.T,
        final_gain.reshape(1, -1),
    )
    return jnp.einsum(
        "rcl,cp->rlp", activated, embed_weight, preferred_element_type=F32
    ).astype(BF16)


def solution(mesh):
    return jax.shard_map(
        local,
        mesh=mesh,
        in_specs=(P(None, None, ("row", "col"), None), P(("row", "col"), None), *[P()] * 11),
        out_specs=P(("row", "col"), None, None),
        check_vma=False,
    )
```

```python
import functools

import jax
import jax.numpy as jnp
from jax import lax
from jax.experimental import pallas as pl
from jax.experimental.pallas import tpu as pltpu
from jax.sharding import PartitionSpec as P

EPSILON = 1e-05
MESH = pl.DeviceIdType.MESH
F32, BF16 = jnp.float32, jnp.bfloat16
Z = 8
ROWS = 5
L = 1280
LANES = 256
BLOCKS = L // LANES
WIDE = 640
HALVES = L // WIDE


def device_at(plane, z, core):
    row = ((plane & 2) << 2) + (z & (Z - 1))
    return (row, (plane & 12) + ((plane & 1) << 1) + core)


def column(row_vector):
    n = row_vector.shape[1]
    rows = lax.broadcasted_iota(jnp.int32, (n, n), 0)
    lanes = lax.broadcasted_iota(jnp.int32, (n, n), 1)
    return jnp.sum(jnp.where(rows == lanes, row_vector, 0.0), axis=1, keepdims=True)


def norm(values, gain):
    centre = values - jnp.mean(values, axis=-2, keepdims=True)
    spread = jnp.mean(centre * centre, axis=-2, keepdims=True)
    return centre * lax.rsqrt(spread + EPSILON) * gain


def norm_both(values, gain):
    return norm(values.reshape(2, 64, -1), gain).reshape(values.shape)


def dot(a, b):
    return jnp.dot(a, b, preferred_element_type=F32)


def weave(first, second):
    pieces = []
    for g in range(first.shape[0] // 8):
        pieces += [first[8 * g : 8 * g + 8], second[8 * g : 8 * g + 8]]
    return jnp.concatenate(pieces, axis=0)


def unweave(both):
    blocks = both.shape[0] // 8
    pieces = [both[8 * b : 8 * b + 8] for t in range(2) for b in range(t, blocks, 2)]
    return jnp.concatenate(pieces, axis=0)


def columns(half):
    return pl.ds(half * WIDE if isinstance(half, int) else pl.multiple_of(half * WIDE, 128), WIDE)


def whole(ref, sem):
    pltpu.make_async_copy(ref, ref, sem).wait()


def kernel(
    pair,
    pair_mask,
    template_mask,
    in_gain,
    proj_weight,
    gate_weight,
    mid_gain,
    out_weight,
    trans_gain,
    up_weight,
    down_weight,
    final_gain,
    result,
    proj_t,
    out_t,
    up_t,
    down_t,
    gains,
    own_mask,
    forth,
    back,
    gate,
    left_sent,
    right_sent,
    left_mid,
    right_mid,
    left_turned,
    right_turned,
    left_held,
    right_held,
    left_flat,
    tri_flat,
    right_flat,
    right_rows,
    tri_made,
    tri_mid,
    tri_turned,
    tri_held,
    out_held,
    z_left,
    z_right,
    z_tri,
    p_left,
    p_right,
    p_tri,
    across,
    z_out,
    p_out,
    across_out,
    result_sem,
):
    row, col = lax.axis_index("row"), lax.axis_index("col")
    z, core = row & (Z - 1), col & 1
    place = (col & 12) + ((row & Z) >> 2) + ((col & 2) >> 1)
    device = row * 16 + col
    group = (z - core) & (Z - 1)
    partner = device_at(place, z + 1 - 2 * core, 1 - core)

    barrier = pltpu.get_barrier_semaphore()
    for step in range(1, Z):
        for other in range(2):
            pl.semaphore_signal(
                barrier, inc=1, device_id=device_at(place, z + step, other), device_id_type=MESH
            )
    pl.semaphore_signal(
        barrier, inc=1, device_id=device_at(place, z, 1 - core), device_id_type=MESH
    )

    def greet(step, carry):
        pl.semaphore_signal(
            barrier,
            inc=1,
            device_id=device_at(lax.bitwise_xor(place, step), z, core),
            device_id_type=MESH,
        )
        return carry

    lax.fori_loop(1, 16, greet, 0)

    proj_t[0:256, :] = jnp.transpose(proj_weight[...].astype(F32)).astype(BF16)
    proj_t[256:320, :] = jnp.transpose(gate_weight[...].astype(F32)).astype(BF16)
    out_t[...] = jnp.zeros_like(out_t)
    up_t[...] = jnp.zeros_like(up_t)
    down_t[...] = jnp.zeros_like(down_t)
    for t in range(2):
        own, wide = pl.ds(64 * t, 64), pl.ds(128 * t, 128)
        out_t[own, own] = jnp.transpose(out_weight[...].astype(F32)).astype(BF16)
        up_t[wide, own] = jnp.transpose(up_weight[...].astype(F32)).astype(BF16)
        down_t[own, wide] = down_weight[...]
    for n, vector in enumerate((in_gain, mid_gain, trans_gain, final_gain)):
        gains[n] = column(vector[...])
    lanes = lax.broadcasted_iota(jnp.int32, (2, L), 1)
    for r in range(ROWS):
        own_mask[r] = jnp.sum(
            jnp.where(lanes == device * ROWS + r, template_mask[...].astype(F32), 0.0),
            axis=1,
            keepdims=True,
        )
    at = lax.broadcasted_iota(jnp.int32, (128, 128), 0)
    of = lax.broadcasted_iota(jnp.int32, (128, 128), 1)
    forth[...] = jnp.where(of == (at % 8) * 16 + at // 8, 1.0, 0.0).astype(BF16)
    back[...] = jnp.where(of == (at % 16) * 8 + at // 16, 1.0, 0.0).astype(BF16)

    def make(r):
        for block in range(BLOCKS):
            span = pl.ds(block * LANES, LANES)
            mask = pair_mask[pl.ds(r, 1), span].astype(F32)
            lefts, rights, gates = [], [], []
            for t in range(2):
                normed = norm(pair[t, r, :, span].astype(F32), gains[0]).astype(BF16)
                projected = dot(proj_t[...], normed)
                lefts.append(jax.nn.sigmoid(projected[64:128]) * projected[0:64] * mask)
                rights.append(jax.nn.sigmoid(projected[192:256]) * projected[128:192] * mask)
                gates.append(jax.nn.sigmoid(projected[256:320]))
            right_sent[r, :, span] = weave(*rights).astype(BF16)
            left_sent[r, :, span] = weave(*lefts).astype(BF16)
            gate[r, :, span] = jnp.concatenate(gates, axis=0)

    def send_z(r, sent, mid, recv, span=pl.ds(0, L)):
        def send(g, slot, where):
            pltpu.make_async_remote_copy(
                sent.at[r, pl.ds(pl.multiple_of(g * 16, 16), 16), span],
                mid.at[r, pl.ds(pl.multiple_of(slot * 16, 16), 16), span],
                z_out,
                recv,
                device_id=where,
                device_id_type=MESH,
            ).start()

        for m in (3, 2, 1):
            send((z + m) & (Z - 1), (3 - m) * 2 + core, device_at(place, z + m, 0))
            send((z + 7 - m) & (Z - 1), m * 2 + core, device_at(place, z - m, 1))
        send((z + 7 + core) & (Z - 1), 6 * core + core, device_at(place, z, 1 - core))
        pltpu.make_async_copy(
            sent.at[r, pl.ds(pl.multiple_of(group * 16, 16), 16), span],
            mid.at[r, pl.ds(pl.multiple_of((6 - 5 * core) * 16, 16), 16), span],
            recv,
        ).start()

    def send_plane(r, turned, held, recv, span=pl.ds(0, L)):
        def send(step, carry):
            other = lax.bitwise_xor(place, step)
            pltpu.make_async_remote_copy(
                turned.at[r, other, :, span],
                held.at[r, place, :, span],
                p_out,
                recv,
                device_id=device_at(other, z, core),
                device_id_type=MESH,
            ).start()
            return carry

        lax.fori_loop(1, 16, send, 0)
        pltpu.make_async_copy(
            turned.at[r, place, :, span], held.at[r, place, :, span], recv
        ).start()

    def turn(r, mid, turned, span):
        moved = dot(forth[...], mid[r, :, span])
        turned[r, :, :, span] = moved.reshape(16, 8, -1).astype(BF16)

    def turn_back(r, span):
        value = tri_mid[r, :, :, span].astype(F32).reshape(128, -1).astype(BF16)
        tri_turned[r, :, span] = dot(back[...], value).astype(BF16)

    def send_back(r, span, recv):
        def send(slot, where):
            pltpu.make_async_remote_copy(
                tri_turned.at[r, pl.ds(pl.multiple_of(slot * 16, 16), 16), span],
                tri_held.at[r, pl.ds(pl.multiple_of(group * 16, 16), 16), span],
                z_out,
                recv,
                device_id=where,
                device_id_type=MESH,
            ).start()

        for m in (3, 2, 1):
            for other in range(2):
                slot = ((3 - m) + core * (2 * m - 3)) * 2 + other
                send(slot, device_at(place, z - m + 2 * m * core, other))
        send(7 - 7 * core, device_at(place, z, 1 - core))
        pltpu.make_async_copy(
            tri_turned.at[r, pl.ds(pl.multiple_of((6 - 5 * core) * 16, 16), 16), span],
            tri_held.at[r, pl.ds(pl.multiple_of(group * 16, 16), 16), span],
            recv,
        ).start()

    def exchange(r):
        return pltpu.make_async_remote_copy(
            right_held.at[core, r],
            right_held.at[core, r],
            across_out,
            across.at[r],
            device_id=partner,
            device_id_type=MESH,
        )

    def send_right(r, carry):
        make(r)

        @pl.when(r == 0)
        def _():
            pl.semaphore_wait(barrier, 30)

        send_z(r, right_sent, right_mid, z_right.at[r])
        return carry

    def pass_right(r, carry):
        whole(right_mid.at[r], z_right.at[r])
        for half in range(HALVES):
            turn(r, right_mid, right_turned, columns(half))
        send_plane(r, right_turned, right_held.at[core], p_right.at[r])
        return carry

    def give_right(r, carry):
        whole(right_held.at[core, r], p_right.at[r])
        exchange(r).start()
        return carry

    def pass_left(r, carry):
        for half in range(HALVES):
            span = columns(half)
            whole(left_mid.at[r, :, span], z_left.at[r, half])
            turn(r, left_mid, left_turned, span)
            send_plane(r, left_turned, left_held, p_left.at[r], span)
        return carry

    def flatten(r, carry):
        whole(right_held.at[1 - core, r], across.at[r])
        for side in range(2):
            for block in range(BLOCKS):
                span = pl.ds(block * LANES, LANES)
                value = right_held[side, r, :, :, span].astype(F32).reshape(128, LANES)
                start = pl.multiple_of((side * ROWS + r) * 128, 128)
                right_flat[pl.ds(start, 128), span] = value.astype(BF16)
        return carry

    def order(block, carry):
        held = lax.broadcasted_iota(jnp.int32, (1, L), 1)
        chunk = held >> 7
        side = jnp.where(chunk >= ROWS, 1, 0)
        r = chunk - ROWS * side
        source = (held >> 3) & 15
        source_z = (group + 5 + ((held >> 1) & 3) + 4 * side) & 7
        x, y = source >> 2, source & 3
        owner = (((y >> 1) * Z + source_z) * 4 + x) * 4 + (y & 1) * 2 + (held & 1)
        natural = owner * ROWS + r
        start = pl.multiple_of(block * LANES, LANES)
        rows = lax.broadcasted_iota(jnp.int32, (LANES, L), 0) + start
        right_rows[pl.ds(start, LANES), :] = jnp.where(rows == natural, 1.0, 0.0).astype(BF16)
        return carry

    def multiply(r, carry):
        whole(left_held.at[r], p_left.at[r])
        for block in range(BLOCKS):
            span = pl.ds(block * LANES, LANES)
            value = left_held[r, :, :, span].astype(F32).reshape(128, LANES)
            left_flat[:, span] = value.astype(BF16)
        for block in range(BLOCKS):
            span = pl.ds(block * LANES, LANES)
            product = lax.dot_general(
                left_flat[...],
                right_flat[span, :],
                (((1,), (1,)), ((), ())),
                preferred_element_type=F32,
            )
            tri_flat[:, span] = product.astype(BF16)
        for half in range(HALVES):
            span = columns(half)
            moved = lax.dot_general(
                tri_flat[...],
                right_rows[span, :],
                (((1,), (1,)), ((), ())),
                preferred_element_type=F32,
            )
            tri_made[r, :, :, span] = moved.reshape(16, 8, WIDE).astype(BF16)
            send_plane(r, tri_made, tri_mid, p_tri.at[r, half], span)
        return carry

    def give_back(r, carry):
        for half in range(HALVES):
            span = columns(half)
            whole(tri_mid.at[r, :, :, span], p_tri.at[r, half])
            turn_back(r, span)
            send_back(r, span, z_tri.at[r, half])
        return carry

    def finish(r, carry):
        for half in range(HALVES):
            span = columns(half)
            whole(tri_held.at[r, :, span], z_tri.at[r, half])
            triangle = unweave(tri_held[r, :, span].astype(F32))
            pairs = jnp.concatenate([pair[t, r, :, span].astype(F32) for t in range(2)], axis=0)
            tri_normed = norm_both(triangle, gains[1]).astype(BF16)
            updated = pairs + gate[r, :, span] * dot(out_t[...], tri_normed)
            trans_in = norm_both(updated, gains[2]).astype(BF16)
            hidden = jnp.maximum(dot(up_t[...], trans_in), 0.0).astype(BF16)
            final = norm_both(updated + dot(down_t[...], hidden), gains[3])
            coverage = own_mask[r] * template_mask[:, span].astype(F32)
            total = coverage[0:1] * final[0:64] + coverage[1:2] * final[64:128]
            averaged = total / jnp.maximum(coverage[0:1] + coverage[1:2], 1.0)
            out_held[r, :, span] = jnp.maximum(averaged, 0.0).astype(BF16)
            pltpu.make_async_copy(
                out_held.at[r, :, span], result.at[r, :, span], result_sem.at[r]
            ).start()
        return carry

    lax.fori_loop(0, ROWS, send_right, 0)

    def send_left(r):
        for half in range(HALVES):
            send_z(r, left_sent, left_mid, z_left.at[r, half], columns(half))

    def right_step(r, carry):
        pass_right(r, 0)

        @pl.when(r == 4)
        def _():
            for first in [0]:
                send_left(first)

        @pl.when(r > 0)
        def _():
            give_right(r - 1, 0)

        return carry

    lax.fori_loop(0, BLOCKS, order, 0)
    lax.fori_loop(0, ROWS, right_step, 0)
    give_right(ROWS - 1, 0)
    send_left(1)
    pass_left(0, 0)
    send_left(2)
    lax.fori_loop(0, ROWS, flatten, 0)

    def step(s, carry):
        pass_left(s, 0)
        send_left(s + 2)
        multiply(s - 1, 0)
        return carry

    lax.fori_loop(1, ROWS - 2, step, 0)
    pass_left(ROWS - 2, 0)
    give_back(0, 0)
    multiply(ROWS - 3, 0)
    pass_left(ROWS - 1, 0)
    give_back(1, 0)
    multiply(ROWS - 2, 0)
    give_back(2, 0)
    multiply(ROWS - 1, 0)
    give_back(3, 0)
    give_back(4, 0)
    lax.fori_loop(0, ROWS, finish, 0)

    def left_by_now(r, carry):
        for sent in (left_sent, right_sent, tri_turned):
            whole(sent.at[r, pl.ds(0, 112)], z_out)
        for turned in (left_turned, right_turned, tri_made):
            whole(turned.at[r, pl.ds(0, 15)], p_out)
        whole(right_held.at[core, r], across_out)
        pltpu.make_async_copy(out_held.at[r], result.at[r], result_sem.at[r]).wait()
        return carry

    lax.fori_loop(0, ROWS, left_by_now, 0)


def local(template_pair, pair_mask, template_mask, in_gain, proj_weight, gate_weight, mid_gain,
          out_weight, trans_gain, up_weight, down_weight, final_gain, embed_weight):
    flat = (ROWS, 128, L)
    blocks = (ROWS, 16, 8, L)
    dma = pltpu.SemaphoreType.DMA
    vmem = pltpu.VMEM
    activated = pl.pallas_call(
        kernel,
        out_shape=jax.ShapeDtypeStruct((ROWS, 64, L), BF16),
        in_specs=[pl.BlockSpec(memory_space=pltpu.VMEM)] * 12,
        out_specs=pl.BlockSpec(memory_space=pl.ANY),
        scratch_shapes=[
            vmem((320, 64), BF16),
            vmem((128, 128), BF16),
            vmem((256, 128), BF16),
            vmem((128, 256), BF16),
            vmem((4, 64, 1), F32),
            vmem((ROWS, 2, 1), F32),
            vmem((128, 128), BF16),
            vmem((128, 128), BF16),
            vmem((ROWS, 128, L), F32),
            vmem(flat, BF16),
            vmem(flat, BF16),
            vmem(flat, BF16),
            vmem(flat, BF16),
            vmem(blocks, BF16),
            vmem(blocks, BF16),
            vmem(blocks, BF16),
            vmem((2, *blocks), BF16),
            vmem((128, L), BF16),
            vmem((128, L), BF16),
            vmem((L, L), BF16),
            vmem((L, L), BF16),
            vmem(blocks, BF16),
            vmem(blocks, BF16),
            vmem(flat, BF16),
            vmem(flat, BF16),
            vmem((ROWS, 64, L), BF16),
            *[dma((ROWS, HALVES)), dma((ROWS,)), dma((ROWS, HALVES))],
            *[dma((ROWS,)), dma((ROWS,)), dma((ROWS, HALVES)), dma((ROWS,))],
            dma,
            dma,
            dma,
            dma((ROWS,)),
        ],
        compiler_params=pltpu.CompilerParams(
            collective_id=0, has_side_effects=True, vmem_limit_bytes=60 * 2**20
        ),
    )(
        template_pair.transpose(0, 2, 1, 3),
        pair_mask,
        template_mask,
        in_gain.reshape(1, -1),
        proj_weight,
        gate_weight,
        mid_gain.reshape(1, -1),
        out_weight,
        trans_gain.reshape(1, -1),
        up_weight,
        down_weight.T,
        final_gain.reshape(1, -1),
    )
    return jnp.einsum(
        "rcl,cp->rlp", activated, embed_weight, preferred_element_type=F32
    ).astype(BF16)


def solution(mesh):
    return jax.shard_map(
        local,
        mesh=mesh,
        in_specs=(P(None, None, ("row", "col"), None), P(("row", "col"), None), *[P()] * 11),
        out_specs=P(("row", "col"), None, None),
        check_vma=False,
    )
```

```python
import functools

import jax
import jax.numpy as jnp
from jax import lax
from jax.experimental import pallas as pl
from jax.experimental.pallas import tpu as pltpu
from jax.sharding import PartitionSpec as P

EPSILON = 1e-05
MESH = pl.DeviceIdType.MESH
F32, BF16 = jnp.float32, jnp.bfloat16
Z = 8
ROWS = 5
L = 1280
LANES = 256
BLOCKS = L // LANES
WIDE = 640
HALVES = L // WIDE


def device_at(plane, z, core):
    row = ((plane & 2) << 2) + (z & (Z - 1))
    return (row, (plane & 12) + ((plane & 1) << 1) + core)


def column(row_vector):
    n = row_vector.shape[1]
    rows = lax.broadcasted_iota(jnp.int32, (n, n), 0)
    lanes = lax.broadcasted_iota(jnp.int32, (n, n), 1)
    return jnp.sum(jnp.where(rows == lanes, row_vector, 0.0), axis=1, keepdims=True)


def norm(values, gain):
    centre = values - jnp.mean(values, axis=-2, keepdims=True)
    spread = jnp.mean(centre * centre, axis=-2, keepdims=True)
    return centre * lax.rsqrt(spread + EPSILON) * gain


def norm_both(values, gain):
    return norm(values.reshape(2, 64, -1), gain).reshape(values.shape)


def dot(a, b):
    return jnp.dot(a, b, preferred_element_type=F32)


def weave(first, second):
    pieces = []
    for g in range(first.shape[0] // 8):
        pieces += [first[8 * g : 8 * g + 8], second[8 * g : 8 * g + 8]]
    return jnp.concatenate(pieces, axis=0)


def unweave(both):
    blocks = both.shape[0] // 8
    pieces = [both[8 * b : 8 * b + 8] for t in range(2) for b in range(t, blocks, 2)]
    return jnp.concatenate(pieces, axis=0)


def columns(half):
    return pl.ds(half * WIDE if isinstance(half, int) else pl.multiple_of(half * WIDE, 128), WIDE)


def whole(ref, sem):
    pltpu.make_async_copy(ref, ref, sem).wait()


def kernel(
    pair_given,
    pair_mask,
    template_mask,
    in_gain,
    proj_weight,
    gate_weight,
    mid_gain,
    out_weight,
    trans_gain,
    up_weight,
    down_weight,
    final_gain,
    result,
    pair,
    proj_t,
    out_t,
    up_t,
    down_t,
    gains,
    own_mask,
    forth,
    back,
    gate,
    left_sent,
    right_sent,
    left_mid,
    right_mid,
    left_turned,
    right_turned,
    left_held,
    right_held,
    left_flat,
    tri_flat,
    right_flat,
    right_rows,
    tri_made,
    tri_mid,
    tri_turned,
    tri_held,
    out_held,
    z_left,
    z_right,
    z_tri,
    p_left,
    p_right,
    p_tri,
    across,
    z_out,
    p_out,
    across_out,
    result_sem,
    pair_sem,
):
    row, col = lax.axis_index("row"), lax.axis_index("col")
    z, core = row & (Z - 1), col & 1
    place = (col & 12) + ((row & Z) >> 2) + ((col & 2) >> 1)
    device = row * 16 + col
    group = (z - core) & (Z - 1)
    partner = device_at(place, z + 1 - 2 * core, 1 - core)

    def load(r):
        return pltpu.make_async_copy(pair_given.at[:, r], pair.at[:, r], pair_sem.at[r])

    for r in range(ROWS):
        load(r).start()

    barrier = pltpu.get_barrier_semaphore()
    for step in range(1, Z):
        for other in range(2):
            pl.semaphore_signal(
                barrier, inc=1, device_id=device_at(place, z + step, other), device_id_type=MESH
            )
    pl.semaphore_signal(
        barrier, inc=1, device_id=device_at(place, z, 1 - core), device_id_type=MESH
    )

    def greet(step, carry):
        pl.semaphore_signal(
            barrier,
            inc=1,
            device_id=device_at(lax.bitwise_xor(place, step), z, core),
            device_id_type=MESH,
        )
        return carry

    lax.fori_loop(1, 16, greet, 0)

    proj_t[0:256, :] = jnp.transpose(proj_weight[...].astype(F32)).astype(BF16)
    proj_t[256:320, :] = jnp.transpose(gate_weight[...].astype(F32)).astype(BF16)
    gains[0] = column(in_gain[...])

    def make(r):
        load(r).wait()
        for block in range(BLOCKS):
            span = pl.ds(block * LANES, LANES)
            mask = pair_mask[pl.ds(r, 1), span].astype(F32)
            lefts, rights, gates = [], [], []
            for t in range(2):
                normed = norm(pair[t, r, :, span].astype(F32), gains[0]).astype(BF16)
                projected = dot(proj_t[...], normed)
                lefts.append(jax.nn.sigmoid(projected[64:128]) * projected[0:64] * mask)
                rights.append(jax.nn.sigmoid(projected[192:256]) * projected[128:192] * mask)
                gates.append(jax.nn.sigmoid(projected[256:320]))
            right_sent[r, :, span] = weave(*rights).astype(BF16)
            left_sent[r, :, span] = weave(*lefts).astype(BF16)
            gate[r, :, span] = jnp.concatenate(gates, axis=0)

    def send_z(r, sent, mid, recv, span=pl.ds(0, L)):
        def send(g, slot, where):
            pltpu.make_async_remote_copy(
                sent.at[r, pl.ds(pl.multiple_of(g * 16, 16), 16), span],
                mid.at[r, pl.ds(pl.multiple_of(slot * 16, 16), 16), span],
                z_out,
                recv,
                device_id=where,
                device_id_type=MESH,
            ).start()

        for m in (3, 2, 1):
            send((z + m) & (Z - 1), (3 - m) * 2 + core, device_at(place, z + m, 0))
            send((z + 7 - m) & (Z - 1), m * 2 + core, device_at(place, z - m, 1))
        send((z + 7 + core) & (Z - 1), 6 * core + core, device_at(place, z, 1 - core))
        pltpu.make_async_copy(
            sent.at[r, pl.ds(pl.multiple_of(group * 16, 16), 16), span],
            mid.at[r, pl.ds(pl.multiple_of((6 - 5 * core) * 16, 16), 16), span],
            recv,
        ).start()

    def send_plane(r, turned, held, recv, span=pl.ds(0, L)):
        def send(step, carry):
            other = lax.bitwise_xor(place, step)
            pltpu.make_async_remote_copy(
                turned.at[r, other, :, span],
                held.at[r, place, :, span],
                p_out,
                recv,
                device_id=device_at(other, z, core),
                device_id_type=MESH,
            ).start()
            return carry

        lax.fori_loop(1, 16, send, 0)
        pltpu.make_async_copy(
            turned.at[r, place, :, span], held.at[r, place, :, span], recv
        ).start()

    def turn(r, mid, turned, span):
        moved = dot(forth[...], mid[r, :, span])
        turned[r, :, :, span] = moved.reshape(16, 8, -1).astype(BF16)

    def turn_back(r, span):
        value = tri_mid[r, :, :, span].astype(F32).reshape(128, -1).astype(BF16)
        tri_turned[r, :, span] = dot(back[...], value).astype(BF16)

    def send_back(r, span, recv):
        def send(slot, where):
            pltpu.make_async_remote_copy(
                tri_turned.at[r, pl.ds(pl.multiple_of(slot * 16, 16), 16), span],
                tri_held.at[r, pl.ds(pl.multiple_of(group * 16, 16), 16), span],
                z_out,
                recv,
                device_id=where,
                device_id_type=MESH,
            ).start()

        for m in (3, 2, 1):
            for other in range(2):
                slot = ((3 - m) + core * (2 * m - 3)) * 2 + other
                send(slot, device_at(place, z - m + 2 * m * core, other))
        send(7 - 7 * core, device_at(place, z, 1 - core))
        pltpu.make_async_copy(
            tri_turned.at[r, pl.ds(pl.multiple_of((6 - 5 * core) * 16, 16), 16), span],
            tri_held.at[r, pl.ds(pl.multiple_of(group * 16, 16), 16), span],
            recv,
        ).start()

    def exchange(r):
        return pltpu.make_async_remote_copy(
            right_held.at[core, r],
            right_held.at[core, r],
            across_out,
            across.at[r],
            device_id=partner,
            device_id_type=MESH,
        )

    def send_right(r, carry):
        make(r)

        @pl.when(r == 0)
        def _():
            pl.semaphore_wait(barrier, 30)

        send_z(r, right_sent, right_mid, z_right.at[r])
        return carry

    def pass_right(r, carry):
        whole(right_mid.at[r], z_right.at[r])
        for half in range(HALVES):
            turn(r, right_mid, right_turned, columns(half))
        send_plane(r, right_turned, right_held.at[core], p_right.at[r])
        return carry

    def give_right(r, carry):
        whole(right_held.at[core, r], p_right.at[r])
        exchange(r).start()
        return carry

    def pass_left(r, carry):
        for half in range(HALVES):
            span = columns(half)
            whole(left_mid.at[r, :, span], z_left.at[r, half])
            turn(r, left_mid, left_turned, span)
            send_plane(r, left_turned, left_held, p_left.at[r], span)
        return carry

    def flatten(r, carry):
        whole(right_held.at[1 - core, r], across.at[r])
        for side in range(2):
            for block in range(BLOCKS):
                span = pl.ds(block * LANES, LANES)
                value = right_held[side, r, :, :, span].astype(F32).reshape(128, LANES)
                start = pl.multiple_of((side * ROWS + r) * 128, 128)
                right_flat[pl.ds(start, 128), span] = value.astype(BF16)
        return carry

    def order(block, carry):
        held = lax.broadcasted_iota(jnp.int32, (1, L), 1)
        chunk = held >> 7
        side = jnp.where(chunk >= ROWS, 1, 0)
        r = chunk - ROWS * side
        source = (held >> 3) & 15
        source_z = (group + 5 + ((held >> 1) & 3) + 4 * side) & 7
        x, y = source >> 2, source & 3
        owner = (((y >> 1) * Z + source_z) * 4 + x) * 4 + (y & 1) * 2 + (held & 1)
        natural = owner * ROWS + r
        start = pl.multiple_of(block * LANES, LANES)
        rows = lax.broadcasted_iota(jnp.int32, (LANES, L), 0) + start
        right_rows[pl.ds(start, LANES), :] = jnp.where(rows == natural, 1.0, 0.0).astype(BF16)
        return carry

    def multiply(r, carry):
        whole(left_held.at[r], p_left.at[r])
        for block in range(BLOCKS):
            span = pl.ds(block * LANES, LANES)
            value = left_held[r, :, :, span].astype(F32).reshape(128, LANES)
            left_flat[:, span] = value.astype(BF16)
        for block in range(BLOCKS):
            span = pl.ds(block * LANES, LANES)
            product = lax.dot_general(
                left_flat[...],
                right_flat[span, :],
                (((1,), (1,)), ((), ())),
                preferred_element_type=F32,
            )
            tri_flat[:, span] = product.astype(BF16)
        for half in range(HALVES):
            span = columns(half)
            moved = lax.dot_general(
                tri_flat[...],
                right_rows[span, :],
                (((1,), (1,)), ((), ())),
                preferred_element_type=F32,
            )
            tri_made[r, :, :, span] = moved.reshape(16, 8, WIDE).astype(BF16)
            send_plane(r, tri_made, tri_mid, p_tri.at[r, half], span)
        return carry

    def give_back(r, carry):
        for half in range(HALVES):
            span = columns(half)
            whole(tri_mid.at[r, :, :, span], p_tri.at[r, half])
            turn_back(r, span)
            send_back(r, span, z_tri.at[r, half])
        return carry

    def finish(r, carry):
        for half in range(HALVES):
            span = columns(half)
            whole(tri_held.at[r, :, span], z_tri.at[r, half])
            triangle = unweave(tri_held[r, :, span].astype(F32))
            pairs = jnp.concatenate([pair[t, r, :, span].astype(F32) for t in range(2)], axis=0)
            tri_normed = norm_both(triangle, gains[1]).astype(BF16)
            updated = pairs + gate[r, :, span] * dot(out_t[...], tri_normed)
            trans_in = norm_both(updated, gains[2]).astype(BF16)
            hidden = jnp.maximum(dot(up_t[...], trans_in), 0.0).astype(BF16)
            final = norm_both(updated + dot(down_t[...], hidden), gains[3])
            coverage = own_mask[r] * template_mask[:, span].astype(F32)
            total = coverage[0:1] * final[0:64] + coverage[1:2] * final[64:128]
            averaged = total / jnp.maximum(coverage[0:1] + coverage[1:2], 1.0)
            out_held[r, :, span] = jnp.maximum(averaged, 0.0).astype(BF16)
            pltpu.make_async_copy(
                out_held.at[r, :, span], result.at[r, :, span], result_sem.at[r]
            ).start()
        return carry

    lax.fori_loop(0, ROWS, send_right, 0)

    def send_left(r):
        for half in range(HALVES):
            send_z(r, left_sent, left_mid, z_left.at[r, half], columns(half))

    def right_step(r, carry):
        pass_right(r, 0)

        @pl.when(r == ROWS - 1)
        def _():
            send_left(0)

        @pl.when(r > 0)
        def _():
            give_right(r - 1, 0)

        return carry

    out_t[...] = jnp.zeros_like(out_t)
    up_t[...] = jnp.zeros_like(up_t)
    down_t[...] = jnp.zeros_like(down_t)
    for t in range(2):
        own, wide = pl.ds(64 * t, 64), pl.ds(128 * t, 128)
        out_t[own, own] = jnp.transpose(out_weight[...].astype(F32)).astype(BF16)
        up_t[wide, own] = jnp.transpose(up_weight[...].astype(F32)).astype(BF16)
        down_t[own, wide] = down_weight[...]
    for n, vector in enumerate((mid_gain, trans_gain, final_gain)):
        gains[n + 1] = column(vector[...])
    lanes = lax.broadcasted_iota(jnp.int32, (2, L), 1)
    for r in range(ROWS):
        own_mask[r] = jnp.sum(
            jnp.where(lanes == device * ROWS + r, template_mask[...].astype(F32), 0.0),
            axis=1,
            keepdims=True,
        )
    at = lax.broadcasted_iota(jnp.int32, (128, 128), 0)
    of = lax.broadcasted_iota(jnp.int32, (128, 128), 1)
    forth[...] = jnp.where(of == (at % 8) * 16 + at // 8, 1.0, 0.0).astype(BF16)
    back[...] = jnp.where(of == (at % 16) * 8 + at // 16, 1.0, 0.0).astype(BF16)
    lax.fori_loop(0, BLOCKS, order, 0)
    lax.fori_loop(0, ROWS, right_step, 0)
    give_right(ROWS - 1, 0)
    send_left(1)
    pass_left(0, 0)
    send_left(2)
    lax.fori_loop(0, ROWS, flatten, 0)

    def step(s, carry):
        pass_left(s, 0)
        send_left(s + 2)
        multiply(s - 1, 0)
        return carry

    lax.fori_loop(1, ROWS - 2, step, 0)
    pass_left(ROWS - 2, 0)
    give_back(0, 0)
    multiply(ROWS - 3, 0)
    pass_left(ROWS - 1, 0)
    give_back(1, 0)
    multiply(ROWS - 2, 0)
    give_back(2, 0)
    multiply(ROWS - 1, 0)
    give_back(3, 0)
    give_back(4, 0)
    lax.fori_loop(0, ROWS, finish, 0)

    def left_by_now(r, carry):
        for sent in (left_sent, right_sent, tri_turned):
            whole(sent.at[r, pl.ds(0, 112)], z_out)
        for turned in (left_turned, right_turned, tri_made):
            whole(turned.at[r, pl.ds(0, 15)], p_out)
        whole(right_held.at[core, r], across_out)
        pltpu.make_async_copy(out_held.at[r], result.at[r], result_sem.at[r]).wait()
        return carry

    lax.fori_loop(0, ROWS, left_by_now, 0)


def local(template_pair, pair_mask, template_mask, in_gain, proj_weight, gate_weight, mid_gain,
          out_weight, trans_gain, up_weight, down_weight, final_gain, embed_weight):
    flat = (ROWS, 128, L)
    blocks = (ROWS, 16, 8, L)
    dma = pltpu.SemaphoreType.DMA
    vmem = pltpu.VMEM
    activated = pl.pallas_call(
        kernel,
        out_shape=jax.ShapeDtypeStruct((ROWS, 64, L), BF16),
        in_specs=[
            pl.BlockSpec(memory_space=pl.ANY),
            *[pl.BlockSpec(memory_space=pltpu.VMEM)] * 11,
        ],
        out_specs=pl.BlockSpec(memory_space=pl.ANY),
        scratch_shapes=[
            vmem((2, ROWS, 64, L), BF16),
            vmem((320, 64), BF16),
            vmem((128, 128), BF16),
            vmem((256, 128), BF16),
            vmem((128, 256), BF16),
            vmem((4, 64, 1), F32),
            vmem((ROWS, 2, 1), F32),
            vmem((128, 128), BF16),
            vmem((128, 128), BF16),
            vmem((ROWS, 128, L), F32),
            vmem(flat, BF16),
            vmem(flat, BF16),
            vmem(flat, BF16),
            vmem(flat, BF16),
            vmem(blocks, BF16),
            vmem(blocks, BF16),
            vmem(blocks, BF16),
            vmem((2, *blocks), BF16),
            vmem((128, L), BF16),
            vmem((128, L), BF16),
            vmem((L, L), BF16),
            vmem((L, L), BF16),
            vmem(blocks, BF16),
            vmem(blocks, BF16),
            vmem(flat, BF16),
            vmem(flat, BF16),
            vmem((ROWS, 64, L), BF16),
            *[dma((ROWS, HALVES)), dma((ROWS,)), dma((ROWS, HALVES))],
            *[dma((ROWS,)), dma((ROWS,)), dma((ROWS, HALVES)), dma((ROWS,))],
            dma,
            dma,
            dma,
            dma((ROWS,)),
            dma((ROWS,)),
        ],
        compiler_params=pltpu.CompilerParams(
            collective_id=0, has_side_effects=True, vmem_limit_bytes=60 * 2**20
        ),
    )(
        template_pair.transpose(0, 2, 1, 3),
        pair_mask,
        template_mask,
        in_gain.reshape(1, -1),
        proj_weight,
        gate_weight,
        mid_gain.reshape(1, -1),
        out_weight,
        trans_gain.reshape(1, -1),
        up_weight,
        down_weight.T,
        final_gain.reshape(1, -1),
    )
    return jnp.einsum(
        "rcl,cp->rlp", activated, embed_weight, preferred_element_type=F32
    ).astype(BF16)


def solution(mesh):
    return jax.shard_map(
        local,
        mesh=mesh,
        in_specs=(P(None, None, ("row", "col"), None), P(("row", "col"), None), *[P()] * 11),
        out_specs=P(("row", "col"), None, None),
        check_vma=False,
    )
```

```python
import functools

import jax
import jax.numpy as jnp
from jax import lax
from jax.experimental import pallas as pl
from jax.experimental.pallas import tpu as pltpu
from jax.sharding import PartitionSpec as P

EPSILON = 1e-05
MESH = pl.DeviceIdType.MESH
F32, BF16 = jnp.float32, jnp.bfloat16
Z = 8
ROWS = 5
L = 1280
LANES = 256
BLOCKS = L // LANES
WIDE = 640
HALVES = L // WIDE


def device_at(plane, z, core):
    row = ((plane & 2) << 2) + (z & (Z - 1))
    return (row, (plane & 12) + ((plane & 1) << 1) + core)


def column(row_vector):
    n = row_vector.shape[1]
    rows = lax.broadcasted_iota(jnp.int32, (n, n), 0)
    lanes = lax.broadcasted_iota(jnp.int32, (n, n), 1)
    return jnp.sum(jnp.where(rows == lanes, row_vector, 0.0), axis=1, keepdims=True)


def norm(values, gain):
    centre = values - jnp.mean(values, axis=-2, keepdims=True)
    spread = jnp.mean(centre * centre, axis=-2, keepdims=True)
    return centre * lax.rsqrt(spread + EPSILON) * gain


def norm_both(values, gain):
    return norm(values.reshape(2, 64, -1), gain).reshape(values.shape)


def dot(a, b):
    return jnp.dot(a, b, preferred_element_type=F32)


def weave(first, second):
    pieces = []
    for g in range(first.shape[0] // 8):
        pieces += [first[8 * g : 8 * g + 8], second[8 * g : 8 * g + 8]]
    return jnp.concatenate(pieces, axis=0)


def unweave(both):
    blocks = both.shape[0] // 8
    pieces = [both[8 * b : 8 * b + 8] for t in range(2) for b in range(t, blocks, 2)]
    return jnp.concatenate(pieces, axis=0)


def columns(half):
    return pl.ds(half * WIDE if isinstance(half, int) else pl.multiple_of(half * WIDE, 128), WIDE)


def whole(ref, sem):
    pltpu.make_async_copy(ref, ref, sem).wait()


def kernel(
    pair_given,
    pair_mask,
    template_mask,
    in_gain,
    proj_weight,
    gate_weight,
    mid_gain,
    out_weight,
    trans_gain,
    up_weight,
    down_weight,
    final_gain,
    result,
    pair,
    proj_t,
    out_t,
    up_t,
    down_t,
    gains,
    own_mask,
    forth,
    back,
    gate,
    left_sent,
    right_sent,
    left_mid,
    right_mid,
    left_turned,
    right_turned,
    left_held,
    right_held,
    left_flat,
    tri_flat,
    tri_part,
    right_flat,
    right_rows,
    tri_made,
    tri_mid,
    tri_turned,
    tri_held,
    out_held,
    z_left,
    z_right,
    z_tri,
    p_left,
    p_right,
    p_tri,
    across,
    z_out,
    p_out,
    across_out,
    result_sem,
    pair_sem,
):
    row, col = lax.axis_index("row"), lax.axis_index("col")
    z, core = row & (Z - 1), col & 1
    place = (col & 12) + ((row & Z) >> 2) + ((col & 2) >> 1)
    device = row * 16 + col
    group = (z - core) & (Z - 1)
    partner = device_at(place, z + 1 - 2 * core, 1 - core)

    def load(r):
        return pltpu.make_async_copy(pair_given.at[:, r], pair.at[:, r], pair_sem.at[r])

    for r in range(ROWS):
        load(r).start()

    barrier = pltpu.get_barrier_semaphore()
    for step in range(1, Z):
        for other in range(2):
            pl.semaphore_signal(
                barrier, inc=1, device_id=device_at(place, z + step, other), device_id_type=MESH
            )
    pl.semaphore_signal(
        barrier, inc=1, device_id=device_at(place, z, 1 - core), device_id_type=MESH
    )

    def greet(step, carry):
        pl.semaphore_signal(
            barrier,
            inc=1,
            device_id=device_at(lax.bitwise_xor(place, step), z, core),
            device_id_type=MESH,
        )
        return carry

    lax.fori_loop(1, 16, greet, 0)

    proj_t[0:256, :] = jnp.transpose(proj_weight[...].astype(F32)).astype(BF16)
    proj_t[256:320, :] = jnp.transpose(gate_weight[...].astype(F32)).astype(BF16)
    gains[0] = column(in_gain[...])

    def make(r):
        load(r).wait()
        for block in range(BLOCKS):
            span = pl.ds(block * LANES, LANES)
            mask = pair_mask[pl.ds(r, 1), span].astype(F32)
            lefts, rights, gates = [], [], []
            for t in range(2):
                normed = norm(pair[t, r, :, span].astype(F32), gains[0]).astype(BF16)
                projected = dot(proj_t[...], normed)
                lefts.append(jax.nn.sigmoid(projected[64:128]) * projected[0:64] * mask)
                rights.append(jax.nn.sigmoid(projected[192:256]) * projected[128:192] * mask)
                gates.append(jax.nn.sigmoid(projected[256:320]))
            right_sent[r, :, span] = weave(*rights).astype(BF16)
            left_sent[r, :, span] = weave(*lefts).astype(BF16)
            gate[r, :, span] = jnp.concatenate(gates, axis=0)

    def send_z(r, sent, mid, recv, span=pl.ds(0, L)):
        def send(g, slot, where):
            pltpu.make_async_remote_copy(
                sent.at[r, pl.ds(pl.multiple_of(g * 16, 16), 16), span],
                mid.at[r, pl.ds(pl.multiple_of(slot * 16, 16), 16), span],
                z_out,
                recv,
                device_id=where,
                device_id_type=MESH,
            ).start()

        for m in (3, 2, 1):
            send((z + m) & (Z - 1), (3 - m) * 2 + core, device_at(place, z + m, 0))
            send((z + 7 - m) & (Z - 1), m * 2 + core, device_at(place, z - m, 1))
        send((z + 7 + core) & (Z - 1), 6 * core + core, device_at(place, z, 1 - core))
        pltpu.make_async_copy(
            sent.at[r, pl.ds(pl.multiple_of(group * 16, 16), 16), span],
            mid.at[r, pl.ds(pl.multiple_of((6 - 5 * core) * 16, 16), 16), span],
            recv,
        ).start()

    def send_plane(r, turned, held, recv, span=pl.ds(0, L)):
        def send(step, carry):
            other = lax.bitwise_xor(place, step)
            pltpu.make_async_remote_copy(
                turned.at[r, other, :, span],
                held.at[r, place, :, span],
                p_out,
                recv,
                device_id=device_at(other, z, core),
                device_id_type=MESH,
            ).start()
            return carry

        lax.fori_loop(1, 16, send, 0)
        pltpu.make_async_copy(
            turned.at[r, place, :, span], held.at[r, place, :, span], recv
        ).start()

    def turn(r, mid, turned, span):
        moved = dot(forth[...], mid[r, :, span])
        turned[r, :, :, span] = moved.reshape(16, 8, -1).astype(BF16)

    def turn_back(r, span):
        value = tri_mid[r, :, :, span].astype(F32).reshape(128, -1).astype(BF16)
        tri_turned[r, :, span] = dot(back[...], value).astype(BF16)

    def send_back(r, span, recv):
        def send(slot, where):
            pltpu.make_async_remote_copy(
                tri_turned.at[r, pl.ds(pl.multiple_of(slot * 16, 16), 16), span],
                tri_held.at[r, pl.ds(pl.multiple_of(group * 16, 16), 16), span],
                z_out,
                recv,
                device_id=where,
                device_id_type=MESH,
            ).start()

        for m in (3, 2, 1):
            for other in range(2):
                slot = ((3 - m) + core * (2 * m - 3)) * 2 + other
                send(slot, device_at(place, z - m + 2 * m * core, other))
        send(7 - 7 * core, device_at(place, z, 1 - core))
        pltpu.make_async_copy(
            tri_turned.at[r, pl.ds(pl.multiple_of((6 - 5 * core) * 16, 16), 16), span],
            tri_held.at[r, pl.ds(pl.multiple_of(group * 16, 16), 16), span],
            recv,
        ).start()

    def exchange(r):
        return pltpu.make_async_remote_copy(
            right_held.at[core, r],
            right_held.at[core, r],
            across_out,
            across.at[r],
            device_id=partner,
            device_id_type=MESH,
        )

    def send_right(r, carry):
        make(r)

        @pl.when(r == 0)
        def _():
            pl.semaphore_wait(barrier, 30)

        send_z(r, right_sent, right_mid, z_right.at[r])
        return carry

    def pass_right(r, carry):
        whole(right_mid.at[r], z_right.at[r])
        for half in range(HALVES):
            turn(r, right_mid, right_turned, columns(half))
        send_plane(r, right_turned, right_held.at[core], p_right.at[r])
        return carry

    def give_right(r, carry):
        whole(right_held.at[core, r], p_right.at[r])
        exchange(r).start()
        return carry

    def pass_left(r, carry):
        for half in range(HALVES):
            span = columns(half)
            whole(left_mid.at[r, :, span], z_left.at[r, half])
            turn(r, left_mid, left_turned, span)
            send_plane(r, left_turned, left_held, p_left.at[r, half], span)
        return carry

    def flatten(r, carry):
        whole(right_held.at[1 - core, r], across.at[r])
        for side in range(2):
            for block in range(BLOCKS):
                span = pl.ds(block * LANES, LANES)
                value = right_held[side, r, :, :, span].astype(F32).reshape(128, LANES)
                start = pl.multiple_of((side * ROWS + r) * 128, 128)
                right_flat[pl.ds(start, 128), span] = value.astype(BF16)
        return carry

    def order(block, carry):
        held = lax.broadcasted_iota(jnp.int32, (1, L), 1)
        chunk = held >> 7
        side = jnp.where(chunk >= ROWS, 1, 0)
        r = chunk - ROWS * side
        source = (held >> 3) & 15
        source_z = (group + 5 + ((held >> 1) & 3) + 4 * side) & 7
        x, y = source >> 2, source & 3
        owner = (((y >> 1) * Z + source_z) * 4 + x) * 4 + (y & 1) * 2 + (held & 1)
        natural = owner * ROWS + r
        start = pl.multiple_of(block * LANES, LANES)
        rows = lax.broadcasted_iota(jnp.int32, (LANES, L), 0) + start
        right_rows[pl.ds(start, LANES), :] = jnp.where(rows == natural, 1.0, 0.0).astype(BF16)
        return carry

    def multiply(r, carry):
        for half in range(HALVES):
            span = columns(half)
            whole(left_held.at[r, :, :, span], p_left.at[r, half])
            value = left_held[r, :, :, span].astype(F32).reshape(128, WIDE)
            left_flat[:, span] = value.astype(BF16)
            for block in range(BLOCKS):
                rows = pl.ds(block * LANES, LANES)
                product = lax.dot_general(
                    left_flat[:, span],
                    right_flat[rows, span],
                    (((1,), (1,)), ((), ())),
                    preferred_element_type=F32,
                )
                if half == 0:
                    tri_part[:, rows] = product
                else:
                    tri_flat[:, rows] = (tri_part[:, rows] + product).astype(BF16)
        for half in range(HALVES):
            span = columns(half)
            moved = lax.dot_general(
                tri_flat[...],
                right_rows[span, :],
                (((1,), (1,)), ((), ())),
                preferred_element_type=F32,
            )
            tri_made[r, :, :, span] = moved.reshape(16, 8, WIDE).astype(BF16)
            send_plane(r, tri_made, tri_mid, p_tri.at[r, half], span)
        return carry

    def give_back(r, carry):
        for half in range(HALVES):
            span = columns(half)
            whole(tri_mid.at[r, :, :, span], p_tri.at[r, half])
            turn_back(r, span)
            send_back(r, span, z_tri.at[r, half])
        return carry

    def finish(r, carry):
        for half in range(HALVES):
            span = columns(half)
            whole(tri_held.at[r, :, span], z_tri.at[r, half])
            triangle = unweave(tri_held[r, :, span].astype(F32))
            pairs = jnp.concatenate([pair[t, r, :, span].astype(F32) for t in range(2)], axis=0)
            tri_normed = norm_both(triangle, gains[1]).astype(BF16)
            updated = pairs + gate[r, :, span] * dot(out_t[...], tri_normed)
            trans_in = norm_both(updated, gains[2]).astype(BF16)
            hidden = jnp.maximum(dot(up_t[...], trans_in), 0.0).astype(BF16)
            final = norm_both(updated + dot(down_t[...], hidden), gains[3])
            coverage = own_mask[r] * template_mask[:, span].astype(F32)
            total = coverage[0:1] * final[0:64] + coverage[1:2] * final[64:128]
            averaged = total / jnp.maximum(coverage[0:1] + coverage[1:2], 1.0)
            out_held[r, :, span] = jnp.maximum(averaged, 0.0).astype(BF16)
            pltpu.make_async_copy(
                out_held.at[r, :, span], result.at[r, :, span], result_sem.at[r]
            ).start()
        return carry

    lax.fori_loop(0, ROWS, send_right, 0)

    def send_left(r):
        for half in range(HALVES):
            send_z(r, left_sent, left_mid, z_left.at[r, half], columns(half))

    def right_step(r, carry):
        pass_right(r, 0)

        @pl.when(r == ROWS - 1)
        def _():
            send_left(0)

        @pl.when(r > 0)
        def _():
            give_right(r - 1, 0)

        return carry

    out_t[...] = jnp.zeros_like(out_t)
    up_t[...] = jnp.zeros_like(up_t)
    down_t[...] = jnp.zeros_like(down_t)
    for t in range(2):
        own, wide = pl.ds(64 * t, 64), pl.ds(128 * t, 128)
        out_t[own, own] = jnp.transpose(out_weight[...].astype(F32)).astype(BF16)
        up_t[wide, own] = jnp.transpose(up_weight[...].astype(F32)).astype(BF16)
        down_t[own, wide] = down_weight[...]
    for n, vector in enumerate((mid_gain, trans_gain, final_gain)):
        gains[n + 1] = column(vector[...])
    lanes = lax.broadcasted_iota(jnp.int32, (2, L), 1)
    for r in range(ROWS):
        own_mask[r] = jnp.sum(
            jnp.where(lanes == device * ROWS + r, template_mask[...].astype(F32), 0.0),
            axis=1,
            keepdims=True,
        )
    at = lax.broadcasted_iota(jnp.int32, (128, 128), 0)
    of = lax.broadcasted_iota(jnp.int32, (128, 128), 1)
    forth[...] = jnp.where(of == (at % 8) * 16 + at // 8, 1.0, 0.0).astype(BF16)
    back[...] = jnp.where(of == (at % 16) * 8 + at // 16, 1.0, 0.0).astype(BF16)
    lax.fori_loop(0, BLOCKS, order, 0)
    lax.fori_loop(0, ROWS, right_step, 0)
    give_right(ROWS - 1, 0)
    send_left(1)
    pass_left(0, 0)
    send_left(2)
    lax.fori_loop(0, ROWS, flatten, 0)

    def step(s, carry):
        pass_left(s, 0)
        send_left(s + 2)
        multiply(s - 1, 0)
        return carry

    lax.fori_loop(1, ROWS - 2, step, 0)
    pass_left(ROWS - 2, 0)
    give_back(0, 0)
    multiply(ROWS - 3, 0)
    pass_left(ROWS - 1, 0)
    give_back(1, 0)
    multiply(ROWS - 2, 0)
    give_back(2, 0)
    multiply(ROWS - 1, 0)
    give_back(3, 0)
    give_back(4, 0)
    lax.fori_loop(0, ROWS, finish, 0)

    def left_by_now(r, carry):
        for sent in (left_sent, right_sent, tri_turned):
            whole(sent.at[r, pl.ds(0, 112)], z_out)
        for turned in (left_turned, right_turned, tri_made):
            whole(turned.at[r, pl.ds(0, 15)], p_out)
        whole(right_held.at[core, r], across_out)
        pltpu.make_async_copy(out_held.at[r], result.at[r], result_sem.at[r]).wait()
        return carry

    lax.fori_loop(0, ROWS, left_by_now, 0)


def local(template_pair, pair_mask, template_mask, in_gain, proj_weight, gate_weight, mid_gain,
          out_weight, trans_gain, up_weight, down_weight, final_gain, embed_weight):
    flat = (ROWS, 128, L)
    blocks = (ROWS, 16, 8, L)
    dma = pltpu.SemaphoreType.DMA
    vmem = pltpu.VMEM
    activated = pl.pallas_call(
        kernel,
        out_shape=jax.ShapeDtypeStruct((ROWS, 64, L), BF16),
        in_specs=[
            pl.BlockSpec(memory_space=pl.ANY),
            *[pl.BlockSpec(memory_space=pltpu.VMEM)] * 11,
        ],
        out_specs=pl.BlockSpec(memory_space=pl.ANY),
        scratch_shapes=[
            vmem((2, ROWS, 64, L), BF16),
            vmem((320, 64), BF16),
            vmem((128, 128), BF16),
            vmem((256, 128), BF16),
            vmem((128, 256), BF16),
            vmem((4, 64, 1), F32),
            vmem((ROWS, 2, 1), F32),
            vmem((128, 128), BF16),
            vmem((128, 128), BF16),
            vmem((ROWS, 128, L), F32),
            vmem(flat, BF16),
            vmem(flat, BF16),
            vmem(flat, BF16),
            vmem(flat, BF16),
            vmem(blocks, BF16),
            vmem(blocks, BF16),
            vmem(blocks, BF16),
            vmem((2, *blocks), BF16),
            vmem((128, L), BF16),
            vmem((128, L), BF16),
            vmem((128, L), F32),
            vmem((L, L), BF16),
            vmem((L, L), BF16),
            vmem(blocks, BF16),
            vmem(blocks, BF16),
            vmem(flat, BF16),
            vmem(flat, BF16),
            vmem((ROWS, 64, L), BF16),
            *[dma((ROWS, HALVES)), dma((ROWS,)), dma((ROWS, HALVES))],
            *[dma((ROWS, HALVES)), dma((ROWS,)), dma((ROWS, HALVES)), dma((ROWS,))],
            dma,
            dma,
            dma,
            dma((ROWS,)),
            dma((ROWS,)),
        ],
        compiler_params=pltpu.CompilerParams(
            collective_id=0, has_side_effects=True, vmem_limit_bytes=60 * 2**20
        ),
    )(
        template_pair.transpose(0, 2, 1, 3),
        pair_mask,
        template_mask,
        in_gain.reshape(1, -1),
        proj_weight,
        gate_weight,
        mid_gain.reshape(1, -1),
        out_weight,
        trans_gain.reshape(1, -1),
        up_weight,
        down_weight.T,
        final_gain.reshape(1, -1),
    )
    return jnp.einsum(
        "rcl,cp->rlp", activated, embed_weight, preferred_element_type=F32
    ).astype(BF16)


def solution(mesh):
    return jax.shard_map(
        local,
        mesh=mesh,
        in_specs=(P(None, None, ("row", "col"), None), P(("row", "col"), None), *[P()] * 11),
        out_specs=P(("row", "col"), None, None),
        check_vma=False,
    )
```
